32 devices in a mesh: side: 2 (over x), seq: 4 (over y, core), head: 4 (over z).
Axes of the slice: x: 2, y: 2, z: 4, core: 2. Of those that a mesh axis runs over, the one named last changes fastest.
Arguments:
- cached_hidden: bfloat16 [8, 3072, 8192], P('side', ('seq', 'head')), may hold values from -240 to 240
- page_order: int32 [8, 192], P('side', ('seq', 'head')), may hold values from 0 to 11, as said below
- lengths: int32 [8], P('side'), may hold values from 768 to 3072, as said below
- new_ids: int32 [8, 4], replicated, may hold values from 0 to 64511
- embedding: bfloat16 [64512, 8192], P('side', ('seq', 'head')), may hold values from -128 to 128
- query_proj: bfloat16 [8192, 8192], P(('seq', 'head')), may hold values from -0.15625 to 0.15625
- down_proj: bfloat16 [8192, 1024], P(('seq', 'head')), may hold values from -0.0625 to 0.0625
- key_up: bfloat16 [8, 64, 128], P('head'), may hold values from -0.75 to 0.75
- value_up: bfloat16 [8, 64, 128], P('head'), may hold values from -1.5 to 1.5
- out_proj: bfloat16 [8192, 8192], P('head', 'seq'), may hold values from -0.0625 to 0.0625
Outputs:
- attended: bfloat16 [8, 4, 8192], P('side', None, 'seq')
The draws below stay inside these ranges and needn't reach their ends.
Inputs may be any that keep to these rules, and one draw needn't show every extreme that they name: `lengths`: each request's number of cached tokens; in every draw some request has exactly 3072. `page_order`: in each row every aligned run of 12 entries holds each number once; entry j of run b names the page of run b's 192 positions in which the request's logical page j of that run is stored.
All inputs are finite; a program needn't handle non-finite values.
Results may differ from the reference program's by a relative error of at most 0.012.
The reference program's roundings to bfloat16 on the way count: a program that leaves them out, or rounds other values in their place, can miss the bound.
Values may be sent and summed in bfloat16 or wider, within the bound.
No kernel may reach another device: no remote copies, remote signals or barrier semaphores. Data moves between devices by JAX's collectives and lax.ppermute only.
A program may use at most 128 MiB of HBM per device.

```python
import jax
import jax.numpy as jnp
from jax import lax

D = 8192
HQ = 64
KVH = 8
HD = 128
RANK = 64
VOCAB = 64512
PAGE = 16
NEW = 4
LEN_DEV = 192
REQ = 8
LEN = 3072


def draw_cached_hidden(key, part):
    base_key = jax.random.fold_in(key, 0)
    values = jnp.clip(jax.random.normal(base_key, (REQ, LEN, D), jnp.float32), -6.0, 6.0)
    place = jnp.arange(LEN, dtype=jnp.float32).reshape(1, LEN, 1) / (LEN - 1)
    values = values * 3.0 ** place
    values = jnp.clip(values, -240.0, 240.0)
    return values.astype(jnp.bfloat16)


def draw_page_order(key, part):
    runs = LEN // LEN_DEV
    pages = LEN_DEV // PAGE
    run_keys = jax.random.split(key, REQ * runs)

    def shuffle(one_key):
        return jax.random.permutation(one_key, pages)
    orders = jax.vmap(shuffle)(run_keys)
    return orders.reshape(REQ, runs * pages).astype(jnp.int32)


def draw_lengths(key, part):
    count_key, chosen_key = jax.random.split(jax.random.fold_in(key, 11))
    counts = jax.random.randint(count_key, (REQ,), LEN // 4, LEN + 1)
    chosen = jax.random.randint(chosen_key, (), 0, REQ)
    return jnp.where(jnp.arange(REQ) == chosen, LEN, counts).astype(jnp.int32)


def draw_embedding(key, part):
    base_key, row_key = jax.random.split(key)
    row_scale = 10.0 ** jax.random.uniform(row_key, (VOCAB, 1), jnp.float32)
    column = jnp.arange(D, dtype=jnp.float32) / (D - 1)
    base = jnp.clip(jax.random.normal(base_key, (VOCAB, D), jnp.float32), -5.0, 5.0)
    values = base * row_scale * 3.0 ** column
    values = jnp.clip(values, -128.0, 128.0)
    return values.astype(jnp.bfloat16)


def place_ends(entries, rng, least, largest):
    extent = entries.shape
    spot = [jax.random.randint(jax.random.fold_in(rng, axis), (), 0, extent[axis]) for axis in range(len(extent))]
    entries = entries.at[tuple(spot)].set(least)
    longest = extent.index(max(extent))
    spot[longest] = (spot[longest] + 1) % extent[longest]
    return entries.at[tuple(spot)].set(largest)


def level_of(stream_key, shape, pieces, low, top_value):
    def one(dim, shards_of):
        steps = jax.random.uniform(jax.random.fold_in(jax.random.fold_in(stream_key, 6), dim), (shards_of,), jnp.float32, low / len(pieces), top_value / len(pieces))
        return jnp.repeat(jnp.exp(steps), shape[dim] // shards_of).reshape((-1,) + (1,) * (len(shape) - dim - 1))

    level = one(*pieces[0])
    for cut in pieces[1:]:
        level = level * one(*cut)
    return level


def centred(rng, shape, width, limit, pieces=(), held_as=jnp.bfloat16):
    factor_of = level_of(rng, shape, pieces, -0.22, 0.18) if pieces else 1.0
    drawn = jax.random.normal(rng, shape, jnp.float32) * width * factor_of
    return jnp.minimum(jnp.maximum(drawn, -limit), limit).astype(held_as)


def setup_inputs(seed: int = 0) -> dict:
    key_list = jax.random.split(jax.random.key(seed), 11)
    return {
        "cached_hidden": draw_cached_hidden(jax.random.fold_in(key_list[10], 71), 0),
        "page_order": draw_page_order(jax.random.fold_in(key_list[10], 71), 0),
        "lengths": draw_lengths(jax.random.fold_in(key_list[10], 71), 0),
        "new_ids": place_ends(jax.random.randint(key_list[3], (REQ, NEW), 0, VOCAB), jax.random.fold_in(key_list[3], 1), 0, VOCAB - 1).astype(jnp.int32),
        "embedding": draw_embedding(jax.random.fold_in(key_list[10], 71), 0),
        "query_proj": centred(key_list[5], (D, HQ * HD), (D // 6) ** -0.5, 0.15625, ((0, 16),)),
        "down_proj": centred(key_list[6], (D, KVH * 2 * RANK), D ** -0.5, 0.0625, ((0, 16),)),
        "key_up": centred(key_list[7], (KVH, RANK, HD), RANK ** -0.5, 0.75, ((0, 4),)),
        "value_up": centred(key_list[8], (KVH, RANK, HD), (RANK // 4) ** -0.5, 1.5, ((0, 4),)),
        "out_proj": centred(key_list[9], (HQ * HD, D), (HQ * HD) ** -0.5, 0.0625, ((0, 4), (1, 4))),
    }


rope_base = 500000.0
masked_score = -1e+30

def rotate(values, positions):
    half_width = values.shape[-1] // 2
    frequency = 1.0 / rope_base ** (jnp.arange(half_width, dtype=jnp.float32) * 2.0 / values.shape[-1])
    angles = positions.astype(jnp.float32)[..., None] * frequency
    cosine = jnp.cos(angles)
    sines = jnp.sin(angles)
    lower_half = values[..., :half_width]
    upper_half = values[..., half_width:]
    return jnp.concatenate([lower_half * cosine - upper_half * sines, upper_half * cosine + lower_half * sines], axis=-1)

def settle(values):
    return lax.optimization_barrier(values.astype(jnp.bfloat16))

def rebuild(latent, positions, key_up, value_up):
    key_part = latent[..., :RANK].astype(jnp.float32)
    value_part = latent[..., RANK:].astype(jnp.float32)
    rebuilt_keys = jnp.einsum('pgc,gcd->pgd', key_part, key_up.astype(jnp.float32))
    rebuilt_keys = settle(rotate(rebuilt_keys, positions[:, None]))
    rebuilt_values = settle(jnp.einsum('pgc,gcd->pgd', value_part, value_up.astype(jnp.float32)))
    return (rebuilt_keys, rebuilt_values)

def reference(cached_hidden, page_order, lengths, new_ids, embedding, query_proj, down_proj, key_up, value_up, out_proj):
    group_heads = HQ // KVH
    embedded = jnp.take(embedding, new_ids.reshape(-1), axis=0)
    widened = embedded.astype(jnp.float32)
    inv_rms = lax.rsqrt(lax.optimization_barrier(jnp.mean(widened * widened, axis=-1)) + 1e-05).reshape(REQ, NEW)
    query_raw = jnp.dot(embedded, query_proj, preferred_element_type=jnp.float32).reshape(REQ, NEW, HQ, HD)
    fresh_positions = lengths[:, None] + jnp.arange(NEW, dtype=jnp.int32)[None, :]
    queries = settle(rotate(query_raw * inv_rms[:, :, None, None], fresh_positions[..., None]))
    fresh_raw = jnp.dot(embedded, down_proj, preferred_element_type=jnp.float32).reshape(REQ, NEW, KVH, 2 * RANK)
    fresh_latent = settle(fresh_raw * inv_rms[:, :, None, None])

    def project(hidden_rows):
        return jnp.dot(hidden_rows, down_proj, preferred_element_type=jnp.float32).astype(jnp.bfloat16)
    cached_latent = lax.map(project, cached_hidden)
    position_ids = jnp.arange(LEN, dtype=jnp.int32)
    scaling = 1.0 / HD ** 0.5
    causal = jnp.arange(NEW, dtype=jnp.int32)[:, None] >= jnp.arange(NEW, dtype=jnp.int32)[None, :]

    def attend(request_item):
        latent_rows, order_row, length, query_rows, fresh_rows, fresh_pos = request_item
        physical = position_ids // LEN_DEV * LEN_DEV + jnp.take(order_row, position_ids // PAGE) * PAGE + position_ids % PAGE
        ordered = jnp.take(latent_rows, physical.astype(jnp.int32), axis=0).reshape(LEN, KVH, 2 * RANK)
        cache_keys, cache_values = rebuild(ordered, position_ids, key_up, value_up)
        fresh_keys, fresh_values = rebuild(fresh_rows, fresh_pos, key_up, value_up)
        grouped = query_rows.reshape(NEW, KVH, group_heads, HD).astype(jnp.float32)
        cache_scores = jnp.einsum('tgjd,pgd->tgjp', grouped, cache_keys.astype(jnp.float32)) * scaling
        fresh_scores = jnp.einsum('tgjd,ugd->tgju', grouped, fresh_keys.astype(jnp.float32)) * scaling
        live = (position_ids < length)[None, None, None, :]
        seen = causal[:, None, None, :]
        cache_scores = jnp.where(live, cache_scores, masked_score)
        fresh_scores = jnp.where(seen, fresh_scores, masked_score)
        row_peak = jnp.maximum(lax.optimization_barrier(jnp.max(cache_scores, axis=-1)), lax.optimization_barrier(jnp.max(fresh_scores, axis=-1)))
        cache_weights = jnp.where(live, jnp.exp(cache_scores - row_peak[..., None]), 0.0)
        fresh_weights = jnp.where(seen, jnp.exp(fresh_scores - row_peak[..., None]), 0.0)
        totals = lax.optimization_barrier(jnp.sum(cache_weights, axis=-1)) + lax.optimization_barrier(jnp.sum(fresh_weights, axis=-1))
        summed = jnp.einsum('tgjp,pgd->tgjd', settle(cache_weights).astype(jnp.float32), cache_values.astype(jnp.float32))
        summed = summed + jnp.einsum('tgju,ugd->tgjd', settle(fresh_weights).astype(jnp.float32), fresh_values.astype(jnp.float32))
        return settle(summed / totals[..., None]).reshape(NEW, HQ * HD)
    context = lax.map(attend, (cached_latent, page_order, lengths, queries, fresh_latent, fresh_positions))
    attended = jnp.dot(context.reshape(REQ * NEW, HQ * HD), out_proj, preferred_element_type=jnp.float32)
    return attended.astype(jnp.bfloat16).reshape(REQ, NEW, D)
```

```python
import functools
import math

import jax
import jax.numpy as jnp
from jax import lax
from jax.experimental import pallas as pl
from jax.experimental.pallas import tpu as pltpu
from jax.sharding import PartitionSpec as P

D = 8192
HQ = 64
KVH = 8
HD = 128
RANK = 64
PAGE = 16
FRESH = 16

AXES = ("side", "seq", "head")
rope_base = 500000.0
masked_score = -1e30
BF = jnp.bfloat16
F32 = jnp.float32


def sincos(positions):
    half = HD // 2
    frequency = 1.0 / rope_base ** (jnp.arange(half, dtype=F32) * 2.0 / HD)
    angles = positions.astype(F32)[..., None] * frequency
    cosine, sines = jnp.cos(angles), jnp.sin(angles)
    return (
        jnp.concatenate([cosine, cosine], axis=-1),
        jnp.concatenate([-sines, sines], axis=-1),
    )


class Grid:
    def __init__(self):
        self.sides, self.seqs, self.heads = (lax.axis_size(a) for a in AXES)
        self.ys = self.seqs // 2
        self.side, seq, self.z = (lax.axis_index(a) for a in AXES)
        self.y, self.c = lax.div(seq, 2), lax.rem(seq, 2)

    def send(self, value, side=0, y=0, core=0, head=0):
        pairs = []
        for a in range(self.sides):
            for b in range(self.ys):
                for c in range(2):
                    for d in range(self.heads):
                        to = (
                            (a + side) % self.sides,
                            (b + y) % self.ys,
                            (c + core) % 2,
                            (d + head) % self.heads,
                        )
                        pairs.append((self.flat(a, b, c, d), self.flat(*to)))
        return lax.ppermute(value, AXES, pairs)

    def place(self, dy, dc, dz):
        seq = lax.rem(self.y + self.ys - dy, self.ys) * 2 + (1 - self.c if dc else self.c)
        return seq * self.heads + lax.rem(self.z + self.heads - dz, self.heads)

    def flat(self, a, b, c, d):
        return (a * self.seqs + b * 2 + c) * self.heads + d


def latent_kernel(counts, segments, depth, has_total, hidden_ref, *refs):
    pieces, refs = refs[: len(counts)], refs[len(counts) :]
    if has_total:
        before_ref, refs = refs[0], refs[1:]
    out_ref, hidden_buf, piece_buf, total, sems = refs
    grid = Grid()
    rows = hidden_ref.shape[0]
    whole = len(segments) + len(pieces)
    if has_total:
        load = pltpu.make_async_copy(before_ref, total, sems.at[whole])
        load.start()
    waits = []
    at = 0
    for i, count in enumerate(counts):
        copies = [
            pltpu.make_async_copy(
                pieces[i], piece_buf.at[pl.ds(at, count), :], sems.at[len(segments) + i]
            )
        ]
        inside = 0
        for k, (owner, extent, dy, dc, dz, base, step) in enumerate(segments):
            if owner == i:
                source = grid.place(dy, dc, dz) * depth + base + step * grid.side
                source = pl.multiple_of(source, 128)
                copies.append(
                    pltpu.make_async_copy(
                        hidden_ref.at[:, pl.ds(source, extent)],
                        hidden_buf.at[:, pl.ds(at + inside, extent)],
                        sems.at[k],
                    )
                )
                inside += extent
        for copy in copies:
            copy.start()
        waits.append((copies, at, count))
        at += count
    if has_total:
        load.wait()
    pairs = [waits[i : i + 2] for i in range(0, len(waits), 2)]
    stores = []
    for k, pair in enumerate(pairs):
        for copies, _, _ in pair:
            for copy in copies:
                copy.wait()
        first = pair[0][1]
        span = sum(count for _, _, count in pair)
        last = k == len(pairs) - 1
        tile = rows // 4 if last else rows
        for m in range(rows // tile):
            part = slice(m * tile, (m + 1) * tile)
            term = jnp.dot(
                hidden_buf[part, first : first + span],
                piece_buf[first : first + span, :],
                preferred_element_type=F32,
            )
            total[part, :] = total[part, :] + term if k or has_total else term
            if last:
                store = pltpu.make_async_copy(
                    total.at[pl.ds(m * tile, tile), :],
                    out_ref.at[pl.ds(m * tile, tile), :],
                    sems.at[whole + 1 + m],
                )
                store.start()
                stores.append(store)
    for store in stores:
        store.wait()


def add_latents(hidden, depth, batch, total=None):
    pieces = [piece for piece, _ in batch]
    counts = [piece.shape[0] for piece in pieces]
    segments = [(i, *part) for i, (_, parts) in enumerate(batch) for part in parts]
    deep, columns = sum(counts), pieces[0].shape[1]
    rows = hidden.shape[0]
    operands = [hidden, *pieces]
    if total is not None:
        operands.append(total)
    return pl.pallas_call(
        functools.partial(latent_kernel, counts, segments, depth, total is not None),
        out_shape=jax.ShapeDtypeStruct((rows, columns), F32),
        in_specs=[pl.BlockSpec(memory_space=pl.ANY)] * len(operands),
        out_specs=pl.BlockSpec(memory_space=pl.ANY),
        scratch_shapes=[
            pltpu.VMEM((rows, deep), BF),
            pltpu.VMEM((deep, columns), BF),
            pltpu.VMEM((rows, columns), F32),
            pltpu.SemaphoreType.DMA((len(segments) + len(pieces) + 5,)),
        ],
        compiler_params=pltpu.CompilerParams(vmem_limit_bytes=53 * 1024 * 1024),
        cost_estimate=pl.CostEstimate(
            flops=2 * rows * deep * columns,
            bytes_accessed=2 * deep * (rows + columns) + 8 * rows * columns,
            transcendentals=0,
        ),
        name="latents",
    )(*operands)


def assemble_kernel(layout, *refs):
    ins, outs = refs[: len(layout)], refs[len(layout) :]
    side = lax.axis_index("side")
    for source, (o, at, count, base, step) in zip(ins, layout):
        start = pl.multiple_of(base + step * side, 32)
        outs[o][at : at + count, :] = source[pl.ds(start, count), :]


def assemble(*arrays):
    layout, sources, shapes = [], [], []
    for o, parts in enumerate(arrays):
        at = 0
        for source, count, base, step in parts:
            layout.append((o, at, count, base, step))
            sources.append(source)
            at += count
        shapes.append(jax.ShapeDtypeStruct((at, source.shape[1]), source.dtype))
    return pl.pallas_call(
        functools.partial(assemble_kernel, layout),
        out_shape=shapes,
        name="assemble",
    )(*sources)


def in_three(value):
    high = value.astype(BF).astype(F32)
    middle = (value - high).astype(BF).astype(F32)
    return high, middle, value - high - middle


def attend_kernel(scale, span, lat_ref, fresh_ref, cos_ref, sin_ref, live_ref, query_ref, up_ref, out_ref):
    requests, groups, lanes, _ = query_ref.shape
    blocks = out_ref.shape[0]
    each = groups // blocks
    peaks, totals, summed = [], [], []
    for r in range(requests):
        latent = jnp.concatenate(
            [lat_ref[r * span : (r + 1) * span, :].astype(BF), fresh_ref[r]], axis=0
        )
        cosine, sines = cos_ref[r], sin_ref[r]
        columns, values = [], []
        for g in range(groups):
            at = g * 2 * RANK
            key = jnp.dot(latent[:, at : at + RANK], up_ref[g], preferred_element_type=F32)
            key = (key * cosine + pltpu.roll(key, HD // 2, 1) * sines).astype(BF)
            columns.append(
                lax.dot_general(
                    key, query_ref[r, g], (((1,), (1,)), ((), ())), preferred_element_type=F32
                )
            )
            values.append(latent[:, at + RANK : at + 2 * RANK])
        scores = jnp.concatenate(columns, axis=1) * scale
        live = live_ref[r] > 0
        live = jnp.concatenate([live] * (scores.shape[1] // live.shape[1]), axis=1)
        scores = jnp.where(live, scores, masked_score)
        peak = jnp.max(scores, axis=0, keepdims=True)
        weights = jnp.where(live, jnp.exp(scores - peak), 0.0)
        peaks.append(peak)
        totals.append(jnp.sum(weights, axis=0, keepdims=True))
        summed.append(
            lax.dot_general(
                jnp.concatenate(values, axis=1),
                weights.astype(BF),
                (((0,), (0,)), ((), ())),
                preferred_element_type=F32,
            )
        )
    for b in range(blocks):
        stats = []
        for i in range(each):
            g = b * each + i
            cut = slice(g * lanes, (g + 1) * lanes)
            out_ref[b, i * RANK : (i + 1) * RANK, :] = jnp.concatenate(
                [s[g * RANK : (g + 1) * RANK, cut] for s in summed], axis=1
            ).astype(BF)
            stats += in_three(jnp.concatenate([p[:, cut] for p in peaks], axis=1))
            stats += in_three(jnp.concatenate([t[:, cut] for t in totals], axis=1))
        stats += [jnp.zeros_like(stats[0])] * (16 - len(stats))
        out_ref[b, each * RANK :, :] = jnp.concatenate(stats, axis=0).astype(BF)


def attend(span, latent, fresh, cosine, sines, live, queries, key_up, blocks):
    requests, groups, lanes, _ = queries.shape
    rows = groups // blocks * RANK + 16
    return pl.pallas_call(
        functools.partial(attend_kernel, 1.0 / math.sqrt(HD), span),
        out_shape=jax.ShapeDtypeStruct((blocks, rows, requests * lanes), BF),
        compiler_params=pltpu.CompilerParams(vmem_limit_bytes=28 * 1024 * 1024),
        name="attend",
    )(latent, fresh, cosine, sines, live, queries, key_up)


def join(states):
    peak = functools.reduce(jnp.maximum, [p for p, _, _ in states])
    total, summed = 0.0, 0.0
    for p, t, s in states:
        weight = jnp.exp(p - peak)
        total = total + t * weight
        summed = summed + s * weight
    return peak, total, summed


def pack(states, out_ref):
    each = len(states)
    stats = []
    for i, (peak, total, summed) in enumerate(states):
        out_ref[i * RANK : (i + 1) * RANK, :] = summed
        stats += [peak, total]
    stats += [jnp.zeros_like(stats[0])] * (8 - len(stats))
    out_ref[each * RANK :, :] = jnp.concatenate(stats, axis=0)


def unpack(ref, each):
    at = each * RANK
    return [
        (ref[at + 2 * i : at + 2 * i + 1, :], ref[at + 2 * i + 1 : at + 2 * i + 2, :], ref[i * RANK : (i + 1) * RANK, :])
        for i in range(each)
    ]


def join_narrow_kernel(each, *refs):
    refs, out_ref = refs[:-1], refs[-1]
    states = []
    for i in range(each):
        parts = []
        for ref in refs:
            stats = ref[each * RANK :, :].astype(F32)
            at = 6 * i
            peak = stats[at : at + 1] + stats[at + 1 : at + 2] + stats[at + 2 : at + 3]
            total = stats[at + 3 : at + 4] + stats[at + 4 : at + 5] + stats[at + 5 : at + 6]
            parts.append((peak, total, ref[i * RANK : (i + 1) * RANK, :].astype(F32)))
        states.append(join(parts))
    pack(states, out_ref)


def join_narrow(parts):
    rows, lanes = parts[0].shape
    return pl.pallas_call(
        functools.partial(join_narrow_kernel, (rows - 16) // RANK),
        out_shape=jax.ShapeDtypeStruct((rows - 8, lanes), F32),
        name="join_narrow",
    )(*parts)


def join_wide_kernel(each, *refs):
    refs, out_ref = refs[:-1], refs[-1]
    parts = [unpack(ref, each) for ref in refs]
    pack([join([part[i] for part in parts]) for i in range(each)], out_ref)


def join_wide(parts):
    return pl.pallas_call(
        functools.partial(join_wide_kernel, (parts[0].shape[0] - 8) // RANK),
        out_shape=jax.ShapeDtypeStruct(parts[0].shape, F32),
        name="join_wide",
    )(*parts)


def context_kernel(requests, steps, *refs):
    up_ref, out_ref = refs[-2:]
    each = up_ref.shape[0]
    parts = [unpack(ref, each) for ref in refs[:-2]]
    lanes = refs[0].shape[1]
    rows = requests * steps
    heads = lanes // rows
    old = lax.broadcasted_iota(jnp.int32, (lanes, lanes), 0)
    new = lax.broadcasted_iota(jnp.int32, (lanes, lanes), 1)
    request, rest = old // (heads * steps), old % (heads * steps)
    moved = (rest // steps) * rows + request * steps + rest % steps
    order = jnp.where(moved == new, 1.0, 0.0).astype(BF)
    for i in range(each):
        _, total, summed = join([part[i] for part in parts])
        scaled = (summed / total).astype(BF)
        context = lax.dot_general(
            up_ref[i], scaled, (((0,), (0,)), ((), ())), preferred_element_type=F32
        ).astype(BF)
        context = lax.dot_general(
            order, context, (((0,), (1,)), ((), ())), preferred_element_type=F32
        ).astype(BF)
        for j in range(heads):
            at = (i * heads + j) * HD
            out_ref[:, at : at + HD] = context[j * rows : (j + 1) * rows, :]


def context_of(parts, value_up, requests, steps):
    rows = requests * steps
    columns = value_up.shape[0] * parts[0].shape[1] // rows * HD
    return pl.pallas_call(
        functools.partial(context_kernel, requests, steps),
        out_shape=jax.ShapeDtypeStruct((rows, columns), BF),
        name="context",
    )(*parts, value_up)


def take(stack, index):
    return lax.dynamic_index_in_dim(stack, index, 0, keepdims=False)


def tie(*values):
    leaves, tree = jax.tree.flatten(values)
    arrays = [i for i, leaf in enumerate(leaves) if getattr(leaf, "ndim", 0)]
    for i, leaf in zip(arrays, lax.optimization_barrier([leaves[i] for i in arrays])):
        leaves[i] = leaf
    return jax.tree.unflatten(tree, leaves)


def in_order(parts, mine):
    count = len(parts)
    if count == 2:
        swap = mine == 0
        return jnp.stack([jnp.where(swap, parts[0], parts[1]), jnp.where(swap, parts[1], parts[0])])
    twice = jnp.stack(parts[::-1] * 2)
    return lax.dynamic_slice_in_dim(twice, count - 1 - mine, count, 0)


def local(
    cached_hidden,
    page_order,
    lengths,
    new_ids,
    embedding,
    query_proj,
    down_proj,
    key_up,
    value_up,
    out_proj,
):
    grid = Grid()
    side, y, c, z = grid.side, grid.y, grid.c, grid.z
    ys, heads = grid.ys, grid.heads
    requests, span, width = cached_hidden.shape
    tokens, steps = new_ids.shape
    rows = requests * steps
    depth = down_proj.shape[0]
    hidden = cached_hidden.reshape(requests * span, width)

    def both(piece, *segments):
        placed = [
            [(rows, dy, dc, dz, base, step) for rows, dy, dz, base, step in segments]
            for dc in range(2)
        ]
        return [(piece, placed[0]), (grid.send(piece, core=1), placed[1])]

    def project_shared(own, between):
        b = depth // 4

        def edge(piece):
            return piece, b, 0, piece.shape[0] - b

        (r0,) = assemble([(own, 3 * b, 0, b)])
        r1 = grid.send(r0, head=1)
        y0 = grid.send(own, y=1)
        own_both = both(own, (4 * b, 0, 0, 0, 0))
        extra = between[0](r0)
        r1, y0, own_both, extra = tie(r1, y0, own_both, extra)
        r2 = grid.send(r1, head=1)
        y1 = grid.send(r1, y=1)
        extra = between[1](extra)
        r1, r2, y0, y1, extra = tie(r1, r2, y0, y1, extra)
        r3 = grid.send(r2, head=1)
        y2 = grid.send(r2, y=1)
        (edges,) = assemble([edge(r1), edge(r2), edge(y1)])
        x2 = grid.send(edges, side=1)
        r1_both = both(r1, (3 * b, 0, 1, 0, b))
        y0_both = both(y0, (4 * b, 1, 0, 0, 0))
        latent = add_latents(hidden, depth, own_both + r1_both + y0_both)
        extra = between[2](extra)
        r2, r3, y1, y2, x2, latent, extra = tie(r2, r3, y1, y2, x2, latent, extra)
        last, edges = assemble([(r3, 2 * b, 0, b)], [edge(r3), edge(y2)])
        last, edges, r2, y1 = tie(last, edges, r2, y1)
        y3 = grid.send(last, y=1)
        x3 = grid.send(edges, side=1)
        r2_both = both(r2, (3 * b, 0, 2, 0, b))
        y1_both = both(y1, (3 * b, 1, 1, 0, b))
        latent = add_latents(hidden, depth, r2_both + y1_both, latent)
        extra = between[3](extra)
        r3, y2, x2, x3, y3, latent, extra = tie(r3, y2, x2, x3, y3, latent, extra)
        x4 = grid.send(y3, side=1)
        x2_both = both(
            x2, (b, 0, 1, 3 * b, -3 * b), (b, 0, 2, 3 * b, -3 * b), (b, 1, 1, 3 * b, -3 * b)
        )
        r3_both = both(r3, (3 * b, 0, 3, 0, b))
        y2_both = both(y2, (3 * b, 1, 2, 0, b))
        latent = add_latents(hidden, depth, x2_both + r3_both + y2_both, latent)
        y3_both = both(y3, (2 * b, 1, 3, 0, 2 * b))
        x3_both = both(x3, (b, 0, 3, 3 * b, -3 * b), (b, 1, 2, 3 * b, -3 * b))
        extra = between[4](extra)
        x3_both, y3_both, latent, extra = tie(x3_both, y3_both, latent, extra)
        x4_both = both(x4, (2 * b, 1, 3, 2 * b, -2 * b))
        return add_latents(hidden, depth, x3_both + y3_both + x4_both, latent), extra

    def project_plain(own, between):
        latent, extra = None, own
        ring = own
        for k in range(heads):
            if k:
                ring = grid.send(ring, head=1)
            latent = add_latents(hidden, depth, both(ring, (depth, 0, k, 0, 0)), latent)
            for dy in range(1, ys):
                piece = grid.send(ring, y=dy)
                latent = add_latents(hidden, depth, both(piece, (depth, dy, k, 0, 0)), latent)
        for step in between:
            extra = step(extra)
        return latent, extra

    blocks = 2 * ys * heads
    query_width = query_proj.shape[1] // blocks
    latent_width = down_proj.shape[1] // blocks
    cut = query_width + latent_width

    def embed(after):
        ids, _ = tie(new_ids, after)
        vocab_half = embedding.shape[0]
        local_ids = ids.reshape(-1) - side * vocab_half
        inside = (local_ids >= 0) & (local_ids < vocab_half)
        picked = jnp.take(embedding, jnp.clip(local_ids, 0, vocab_half - 1), axis=0)
        picked = jnp.where(inside[:, None], picked, jnp.zeros_like(picked)).reshape(2, rows, -1)
        embedded = take(picked, side) + grid.send(take(picked, 1 - side), side=1)
        query_part = jnp.dot(embedded, query_proj, preferred_element_type=F32)
        latent_part = jnp.dot(embedded, down_proj, preferred_element_type=F32)
        widened = embedded.astype(F32)
        square_part = jnp.sum(widened * widened, axis=-1)
        packed = jnp.concatenate(
            [
                query_part.reshape(rows, blocks, query_width),
                latent_part.reshape(rows, blocks, latent_width),
                jnp.broadcast_to(square_part[:, None, None], (rows, blocks, 128 - latent_width)),
            ],
            axis=-1,
        ).transpose(1, 0, 2)
        packed = packed.reshape(2, ys, heads, rows, -1)
        packed = take(packed, c) + grid.send(take(packed, 1 - c), core=1)
        kept = take(packed, y)
        for dy in range(1, ys):
            kept = kept + grid.send(take(packed, (y + dy) % ys), y=dy)
        return kept

    def reduce_query(kept):
        mine = take(kept, z)
        for dz in range(1, heads):
            mine = mine + grid.send(take(kept, (z + dz) % heads), head=dz)
        return mine

    def spread_query(mine):
        inv_rms = lax.rsqrt(mine[:, -1:] / D + 1e-05)
        fresh_positions = lengths[:, None] + jnp.arange(steps, dtype=jnp.int32)[None, :]
        cos_new, sin_new = sincos(fresh_positions.reshape(-1))
        raw = (mine[:, :query_width] * inv_rms).reshape(rows, -1, HD)
        turned = jnp.concatenate([raw[..., HD // 2 :], raw[..., : HD // 2]], axis=-1)
        raw = raw * cos_new[:, None, :] + turned * sin_new[:, None, :]
        latent_new = mine[:, query_width : query_width + latent_width] * inv_rms
        block = jnp.concatenate(
            [raw.reshape(rows, -1).astype(BF), latent_new.astype(BF), key_up.reshape(rows, -1)], axis=-1
        )
        return block

    def spread_head(block):
        by_head = in_order([block] + [grid.send(block, head=k) for k in range(1, heads)], z)
        all_key_up = by_head[..., cut:].reshape(KVH, RANK, HD)
        return by_head[..., :cut], all_key_up

    def share_query(state):
        by_head, all_key_up = state
        by_y = in_order([by_head] + [grid.send(by_head, y=k) for k in range(1, ys)], y)
        by_core = in_order([by_y, grid.send(by_y, core=1)], c)
        by_block = by_core.reshape(blocks, rows, cut)
        queries = by_block[..., :query_width].reshape(blocks, requests, steps, -1, HD)
        queries = queries.transpose(1, 0, 3, 2, 4).reshape(requests, KVH, -1, HD)
        fresh = by_block[..., query_width:].transpose(1, 0, 2).reshape(requests, steps, -1)
        fresh = jnp.pad(fresh, ((0, 0), (0, FRESH - steps), (0, 0)))
        return queries, fresh, all_key_up

    pages = page_order.shape[1]
    logical = jnp.arange(pages, dtype=jnp.int32)
    page_of = jnp.sum(
        jnp.where(page_order[:, :, None] == logical[None, None, :], logical[None, :, None], 0), axis=1
    )
    start = ((y * 2 + c) * heads + z) * span
    positions = (
        start + page_of[:, :, None] * PAGE + jnp.arange(PAGE, dtype=jnp.int32)[None, None, :]
    ).reshape(requests, span)
    new_rows = jnp.arange(FRESH, dtype=jnp.int32)
    row_positions = jnp.concatenate(
        [positions, lengths[:, None] + jnp.minimum(new_rows, steps - 1)[None, :]], axis=1
    )
    cosine, sines = sincos(row_positions)
    lanes = max(128, HQ // KVH * steps)
    step_of = jnp.arange(lanes, dtype=jnp.int32) % steps
    holds_new = (y == 0) & (c == 0) & (z == 0)
    new_seen = (new_rows[:, None] <= step_of[None, :]) & holds_new
    live = jnp.concatenate(
        [
            jnp.broadcast_to((positions < lengths[:, None])[:, :, None], (requests, span, lanes)),
            jnp.broadcast_to(new_seen[None], (requests, FRESH, lanes)),
        ],
        axis=1,
    ).astype(F32)

    between = [embed, reduce_query, spread_query, spread_head, share_query]
    shared = ys == 2 and heads == 4 and grid.sides == 2 and depth % 512 == 0
    latent, extra = (project_shared if shared else project_plain)(down_proj, between)
    queries, fresh, all_key_up = extra
    states = attend(span, latent, fresh, cosine, sines, live, queries, all_key_up, heads)
    parts = [take(states, z)]
    for dz in range(1, heads):
        parts.append(grid.send(take(states, (z + dz) % heads), head=dz))
    state = join_narrow(parts)
    state = join_wide([state] + [grid.send(state, y=k) for k in range(1, ys)])
    context = context_of([state, grid.send(state, core=1)], value_up, requests, steps)
    partial_out = jnp.dot(context, out_proj, preferred_element_type=F32)
    sent = partial_out.astype(BF)
    attended = partial_out
    for dz in range(1, heads):
        attended = attended + grid.send(sent, head=dz).astype(F32)
    return attended.astype(BF).reshape(requests, steps, -1)


def solution(mesh):
    return jax.shard_map(
        local,
        mesh=mesh,
        in_specs=(
            P("side", ("seq", "head"), None),
            P("side", ("seq", "head")),
            P("side"),
            P(),
            P("side", ("seq", "head")),
            P(("seq", "head"), None),
            P(("seq", "head"), None),
            P("head", None, None),
            P("head", None, None),
            P("head", "seq"),
        ),
        out_specs=P("side", None, "seq"),
        check_vma=False,
    )
```

```python
import functools
import math

import jax
import jax.numpy as jnp
from jax import lax
from jax.experimental import pallas as pl
from jax.experimental.pallas import tpu as pltpu
from jax.sharding import PartitionSpec as P

D = 8192
HQ = 64
KVH = 8
HD = 128
RANK = 64
PAGE = 16
FRESH = 16

AXES = ("side", "seq", "head")
rope_base = 500000.0
masked_score = -1e30
BF = jnp.bfloat16
F32 = jnp.float32


def sincos(positions):
    half = HD // 2
    frequency = 1.0 / rope_base ** (jnp.arange(half, dtype=F32) * 2.0 / HD)
    angles = positions.astype(F32)[..., None] * frequency
    cosine, sines = jnp.cos(angles), jnp.sin(angles)
    return (
        jnp.concatenate([cosine, cosine], axis=-1),
        jnp.concatenate([-sines, sines], axis=-1),
    )


class Grid:
    def __init__(self):
        self.sides, self.seqs, self.heads = (lax.axis_size(a) for a in AXES)
        self.ys = self.seqs // 2
        self.side, seq, self.z = (lax.axis_index(a) for a in AXES)
        self.y, self.c = lax.div(seq, 2), lax.rem(seq, 2)

    def send(self, value, side=0, y=0, core=0, head=0):
        pairs = []
        for a in range(self.sides):
            for b in range(self.ys):
                for c in range(2):
                    for d in range(self.heads):
                        to = (
                            (a + side) % self.sides,
                            (b + y) % self.ys,
                            (c + core) % 2,
                            (d + head) % self.heads,
                        )
                        pairs.append((self.flat(a, b, c, d), self.flat(*to)))
        return lax.ppermute(value, AXES, pairs)

    def place(self, dy, dc, dz):
        seq = lax.rem(self.y + self.ys - dy, self.ys) * 2 + (1 - self.c if dc else self.c)
        return seq * self.heads + lax.rem(self.z + self.heads - dz, self.heads)

    def flat(self, a, b, c, d):
        return (a * self.seqs + b * 2 + c) * self.heads + d


def accumulate(
    counts, segments, depth, hidden_ref, pieces, before_ref, hidden_buf, piece_buf, total, sems, store=None
):
    grid = Grid()
    rows = hidden_ref.shape[0]
    if before_ref is not None:
        load = pltpu.make_async_copy(before_ref, total, sems.at[len(segments) + len(pieces)])
    waits = []
    at = 0
    for i, count in enumerate(counts):
        copies = [
            pltpu.make_async_copy(
                pieces[i].at[pl.ds(0, count), :],
                piece_buf.at[pl.ds(at, count), :],
                sems.at[len(segments) + i],
            )
        ]
        inside = 0
        for k, (owner, extent, dy, dc, dz, base, step) in enumerate(segments):
            if owner == i:
                source = grid.place(dy, dc, dz) * depth + base + step * grid.side
                source = pl.multiple_of(source, 128)
                copies.append(
                    pltpu.make_async_copy(
                        hidden_ref.at[:, pl.ds(source, extent)],
                        hidden_buf.at[:, pl.ds(at + inside, extent)],
                        sems.at[k],
                    )
                )
                inside += extent
        for copy in copies:
            copy.start()
        if before_ref is not None and i == 1:
            load.start()
        waits.append((copies, at, count))
        at += count
    pairs = [waits[i : i + 2] for i in range(0, len(waits), 2)]
    for k, pair in enumerate(pairs):
        for copies, _, _ in pair:
            for copy in copies:
                copy.wait()
        first = pair[0][1]
        span = sum(count for _, _, count in pair)
        last = k == len(pairs) - 1
        tile = rows // 4 if last and store else rows
        for m in range(rows // tile):
            part = slice(m * tile, (m + 1) * tile)
            term = jnp.dot(
                hidden_buf[part, first : first + span],
                piece_buf[first : first + span, :],
                preferred_element_type=F32,
            )
            if k == 0 and m == 0 and before_ref is not None:
                load.wait()
            total[part, :] = total[part, :] + term if k or before_ref is not None else term
            if last and store:
                store(m, tile)


def latent_kernel(counts, segments, depth, has_total, hidden_ref, *refs):
    pieces, refs = refs[: len(counts)], refs[len(counts) :]
    before_ref = None
    if has_total:
        before_ref, refs = refs[0], refs[1:]
    out_ref, hidden_buf, piece_buf, total, sems, out_sems = refs
    stores = []

    def store(m, tile):
        rows = pl.ds(m * tile, tile)
        copy = pltpu.make_async_copy(total.at[rows, :], out_ref.at[rows, :], out_sems.at[m])
        copy.start()
        stores.append(copy)

    accumulate(
        counts, segments, depth, hidden_ref, pieces, before_ref, hidden_buf, piece_buf, total, sems, store
    )
    for copy in stores:
        copy.wait()


def add_latents(hidden, depth, batch, total=None):
    pieces = [piece for piece, _ in batch]
    counts = [sum(part[0] for part in parts) for _, parts in batch]
    segments = [(i, *part) for i, (_, parts) in enumerate(batch) for part in parts]
    deep, columns = sum(counts), pieces[0].shape[1]
    rows = hidden.shape[0]
    operands = [hidden, *pieces]
    if total is not None:
        operands.append(total)
    return pl.pallas_call(
        functools.partial(latent_kernel, counts, segments, depth, total is not None),
        out_shape=jax.ShapeDtypeStruct((rows, columns), F32),
        in_specs=[pl.BlockSpec(memory_space=pl.ANY)] * len(operands),
        out_specs=pl.BlockSpec(memory_space=pl.ANY),
        scratch_shapes=[
            pltpu.VMEM((rows, deep), BF),
            pltpu.VMEM((deep, columns), BF),
            pltpu.VMEM((rows, columns), F32),
            pltpu.SemaphoreType.DMA((len(segments) + len(pieces) + 1,)),
            pltpu.SemaphoreType.DMA((4,)),
        ],
        compiler_params=pltpu.CompilerParams(vmem_limit_bytes=28 * 1024 * 1024),
        cost_estimate=pl.CostEstimate(flops=1, bytes_accessed=1, transcendentals=0),
        name="latents",
    )(*operands)


def first_piece_kernel(rows, own_ref, up_ref, out_ref, sems):
    side = lax.axis_index("side")
    groups = up_ref.shape[0]
    each = RANK // FRESH
    start = pl.multiple_of(rows * side, 16)
    copies = [
        pltpu.make_async_copy(
            own_ref.at[pl.ds(start, 3 * rows), :], out_ref.at[pl.ds(0, 3 * rows), :], sems.at[0]
        )
    ]
    for k in range(groups * each):
        copies.append(
            pltpu.make_async_copy(
                up_ref.at[k // each, pl.ds(k % each * FRESH, FRESH), :],
                out_ref.at[pl.ds(3 * rows, FRESH), pl.ds(k * HD, HD)],
                sems.at[1 + k],
            )
        )
    for copy in copies:
        copy.start()
    for copy in copies:
        copy.wait()


def first_piece(own, key_up, rows):
    count = key_up.shape[0] * RANK // FRESH
    return pl.pallas_call(
        functools.partial(first_piece_kernel, rows),
        out_shape=jax.ShapeDtypeStruct((3 * rows + FRESH, own.shape[1]), own.dtype),
        in_specs=[pl.BlockSpec(memory_space=pl.ANY)] * 2,
        out_specs=pl.BlockSpec(memory_space=pltpu.VMEM),
        scratch_shapes=[pltpu.SemaphoreType.DMA((1 + count,))],
        compiler_params=pltpu.CompilerParams(vmem_limit_bytes=8 * 1024 * 1024),
        cost_estimate=pl.CostEstimate(flops=1, bytes_accessed=1, transcendentals=0),
        name="first_piece",
    )(own, key_up)


def assemble_kernel(layout, *refs):
    ins, outs, sems = refs[: len(layout)], refs[len(layout) : -1], refs[-1]
    side = lax.axis_index("side")
    copies = []
    for k, (o, at, count, base, step) in enumerate(layout):
        start = pl.multiple_of(base + step * side, 16)
        copies.append(
            pltpu.make_async_copy(
                ins[k].at[pl.ds(start, count), :], outs[o].at[pl.ds(at, count), :], sems.at[k]
            )
        )
        copies[-1].start()
    for copy in copies:
        copy.wait()


def assemble(*arrays):
    layout, sources, shapes = [], [], []
    for o, parts in enumerate(arrays):
        at = 0
        for source, count, base, step in parts:
            layout.append((o, at, count, base, step))
            sources.append(source)
            at += count
        shapes.append(jax.ShapeDtypeStruct((at, source.shape[1]), source.dtype))
    return pl.pallas_call(
        functools.partial(assemble_kernel, layout),
        out_shape=shapes,
        in_specs=[pl.BlockSpec(memory_space=pl.ANY)] * len(sources),
        out_specs=[pl.BlockSpec(memory_space=pltpu.VMEM)] * len(shapes),
        scratch_shapes=[pltpu.SemaphoreType.DMA((len(layout),))],
        compiler_params=pltpu.CompilerParams(vmem_limit_bytes=8 * 1024 * 1024),
        cost_estimate=pl.CostEstimate(flops=1, bytes_accessed=1, transcendentals=0),
        name="assemble",
    )(*sources)


def in_three(value):
    high = value.astype(BF).astype(F32)
    middle = (value - high).astype(BF).astype(F32)
    return high, middle, value - high - middle


def pack_up(key_up):
    groups = key_up.shape[0]
    parts = key_up.reshape(groups, RANK // FRESH, FRESH, HD).transpose(2, 0, 1, 3)
    return parts.reshape(FRESH, -1)


def unpack_up(up_ref, g):
    each = up_ref.shape[2] // (RANK // FRESH * HD)
    at = g % each * (RANK // FRESH)
    parts = [up_ref[g // each, :, (at + i) * HD : (at + i + 1) * HD] for i in range(RANK // FRESH)]
    return jnp.concatenate(parts, axis=0)


def attend_part(scale, span, lat_ref, fresh_ref, cos_ref, sin_ref, live_ref, query_ref, up_ref, out_ref):
    requests, groups, lanes, _ = query_ref.shape
    blocks = out_ref.shape[0]
    each = groups // blocks
    peaks, totals, summed = [], [], []
    ups = [unpack_up(up_ref, g) for g in range(groups)]
    for r in range(requests):
        latent = jnp.concatenate(
            [
                lat_ref[r * span : (r + 1) * span, :].astype(BF),
                jnp.concatenate([fresh_ref[r, p] for p in range(fresh_ref.shape[1])], axis=1),
            ],
            axis=0,
        )
        cosine, sines = cos_ref[r], sin_ref[r]
        columns, values = [], []
        for g in range(groups):
            at = g * 2 * RANK
            key = jnp.dot(latent[:, at : at + RANK], ups[g], preferred_element_type=F32)
            key = (key * cosine + pltpu.roll(key, HD // 2, 1) * sines).astype(BF)
            columns.append(
                lax.dot_general(
                    key, query_ref[r, g], (((1,), (1,)), ((), ())), preferred_element_type=F32
                )
            )
            values.append(latent[:, at + RANK : at + 2 * RANK])
        scores = jnp.concatenate(columns, axis=1) * scale
        live = live_ref[r] > 0
        live = jnp.concatenate([live] * (scores.shape[1] // live.shape[1]), axis=1)
        scores = jnp.where(live, scores, masked_score)
        peak = jnp.max(scores, axis=0, keepdims=True)
        weights = jnp.where(live, jnp.exp(scores - peak), 0.0)
        peaks.append(peak)
        totals.append(jnp.sum(weights, axis=0, keepdims=True))
        summed.append(
            lax.dot_general(
                jnp.concatenate(values, axis=1),
                weights.astype(BF),
                (((0,), (0,)), ((), ())),
                preferred_element_type=F32,
            )
        )
    for b in range(blocks):
        stats = []
        for i in range(each):
            g = b * each + i
            cut = slice(g * lanes, (g + 1) * lanes)
            out_ref[b, i * RANK : (i + 1) * RANK, :] = jnp.concatenate(
                [s[g * RANK : (g + 1) * RANK, cut] for s in summed], axis=1
            ).astype(BF)
            stats += in_three(jnp.concatenate([p[:, cut] for p in peaks], axis=1))
            stats += in_three(jnp.concatenate([t[:, cut] for t in totals], axis=1))
        stats += [jnp.zeros_like(stats[0])] * (16 - len(stats))
        out_ref[b, each * RANK :, :] = jnp.concatenate(stats, axis=0).astype(BF)


def finish_kernel(counts, segments, depth, scale, span, up_row, hidden_ref, *refs):
    pieces, refs = refs[: len(counts)], refs[len(counts) :]
    before_ref, refs = refs[0], refs[1:]
    heads = lax.axis_size("head")
    tables, ups, weight_ref, refs = refs[:5], refs[5 : 5 + heads], refs[5 + heads], refs[6 + heads :]
    out_ref, weight_out, hidden_buf, piece_buf, total = refs[:5]
    held, up_buf, table_sems, weight_sem = refs[5:10], refs[11], refs[12], refs[13]
    sems = refs[10]
    loads = [
        pltpu.make_async_copy(table, buf, table_sems.at[i])
        for i, (table, buf) in enumerate(zip(tables, held))
    ]
    z = lax.axis_index("head")
    for k, up in enumerate(ups):
        place = lax.rem(z + heads - k, heads)
        loads.append(
            pltpu.make_async_copy(
                up.at[pl.ds(up_row, FRESH), :], up_buf.at[place], table_sems.at[len(tables) + k]
            )
        )
    for load in loads:
        load.start()
    accumulate(counts, segments, depth, hidden_ref, pieces, before_ref, hidden_buf, piece_buf, total, sems)
    for load in loads:
        load.wait()
    bring = pltpu.make_async_copy(weight_ref, weight_out, weight_sem)
    bring.start()
    attend_part(scale, span, total, *held, up_buf, out_ref)
    bring.wait()


def finish(span, hidden, depth, batch, total, fresh, cosine, sines, live, queries, ups, up_row, weight, blocks):
    pieces = [piece for piece, _ in batch]
    counts = [sum(part[0] for part in parts) for _, parts in batch]
    segments = [(i, *part) for i, (_, parts) in enumerate(batch) for part in parts]
    deep, columns = sum(counts), pieces[0].shape[1]
    rows = hidden.shape[0]
    requests, groups, lanes, _ = queries.shape
    tables = (fresh, cosine, sines, live, queries)
    far = [pltpu.with_memory_space_constraint(t, pltpu.HBM) for t in (cosine, sines, live)]
    tables = (fresh, *far, queries)
    operands = [hidden, *pieces, total, *tables, *ups, weight]
    state_rows = groups // blocks * RANK + 16
    return pl.pallas_call(
        functools.partial(finish_kernel, counts, segments, depth, 1.0 / math.sqrt(HD), span, up_row),
        out_shape=(
            jax.ShapeDtypeStruct((blocks, state_rows, requests * lanes), BF),
            pltpu.VMEM(weight.shape, weight.dtype),
        ),
        in_specs=[pl.BlockSpec(memory_space=pl.ANY)] * len(operands),
        out_specs=(pl.BlockSpec(memory_space=pltpu.VMEM), pl.BlockSpec(memory_space=pl.ANY)),
        scratch_shapes=[
            pltpu.VMEM((rows, deep), BF),
            pltpu.VMEM((deep, columns), BF),
            pltpu.VMEM((rows, columns), F32),
        ]
        + [pltpu.VMEM(table.shape, table.dtype) for table in tables]
        + [
            pltpu.SemaphoreType.DMA((len(segments) + len(pieces) + 1,)),
            pltpu.VMEM((len(ups), FRESH, ups[0].shape[1]), BF),
            pltpu.SemaphoreType.DMA((len(tables) + len(ups),)),
            pltpu.SemaphoreType.DMA,
        ],
        compiler_params=pltpu.CompilerParams(vmem_limit_bytes=28 * 1024 * 1024),
        cost_estimate=pl.CostEstimate(flops=1, bytes_accessed=1, transcendentals=0),
        name="finish",
    )(*operands)


def join(states):
    peak = functools.reduce(jnp.maximum, [p for p, _, _ in states])
    total, summed = 0.0, 0.0
    for p, t, s in states:
        weight = jnp.exp(p - peak)
        total = total + t * weight
        summed = summed + s * weight
    return peak, total, summed


def pack(states, out_ref):
    each = len(states)
    stats = []
    for i, (peak, total, summed) in enumerate(states):
        out_ref[i * RANK : (i + 1) * RANK, :] = summed.astype(BF)
        stats += [*in_three(peak), *in_three(total)]
    stats += [jnp.zeros_like(stats[0])] * (16 - len(stats))
    out_ref[each * RANK :, :] = jnp.concatenate(stats, axis=0).astype(BF)


def unpack(ref, each):
    stats = ref[each * RANK :, :].astype(F32)
    states = []
    for i in range(each):
        three = [stats[at : at + 1] for at in range(6 * i, 6 * i + 6)]
        peak, total = three[0] + three[1] + three[2], three[3] + three[4] + three[5]
        states.append((peak, total, ref[i * RANK : (i + 1) * RANK, :].astype(F32)))
    return states


def join_parts_kernel(each, *refs):
    refs, out_ref = refs[:-1], refs[-1]
    parts = [unpack(ref, each) for ref in refs]
    pack([join([part[i] for part in parts]) for i in range(each)], out_ref)


def join_parts(parts):
    return pl.pallas_call(
        functools.partial(join_parts_kernel, (parts[0].shape[0] - 16) // RANK),
        out_shape=jax.ShapeDtypeStruct(parts[0].shape, BF),
        compiler_params=pltpu.CompilerParams(vmem_limit_bytes=4 * 1024 * 1024),
        cost_estimate=pl.CostEstimate(flops=1, bytes_accessed=1, transcendentals=0),
        name="join_parts",
    )(*parts)


def project_out_kernel(requests, steps, *refs):
    up_ref, weight_ref, out_ref = refs[-3:]
    each = up_ref.shape[0]
    parts = [unpack(ref, each) for ref in refs[:-3]]
    lanes = refs[0].shape[1]
    rows = requests * steps
    heads = lanes // rows
    old = lax.broadcasted_iota(jnp.int32, (lanes, lanes), 0)
    new = lax.broadcasted_iota(jnp.int32, (lanes, lanes), 1)
    request, rest = old // (heads * steps), old % (heads * steps)
    moved = (rest // steps) * rows + request * steps + rest % steps
    order = jnp.where(moved == new, 1.0, 0.0).astype(BF)
    context = []
    for i in range(each):
        _, total, summed = join([part[i] for part in parts])
        scaled = (summed / total).astype(BF)
        one = lax.dot_general(
            up_ref[i], scaled, (((0,), (0,)), ((), ())), preferred_element_type=F32
        ).astype(BF)
        one = lax.dot_general(
            order, one, (((0,), (1,)), ((), ())), preferred_element_type=F32
        ).astype(BF)
        context += [one[j * rows : (j + 1) * rows, :] for j in range(heads)]
    out_ref[...] = jnp.dot(
        jnp.concatenate(context, axis=1), weight_ref[...], preferred_element_type=F32
    )


def project_out(parts, value_up, out_proj, requests, steps):
    return pl.pallas_call(
        functools.partial(project_out_kernel, requests, steps),
        out_shape=jax.ShapeDtypeStruct((requests * steps, out_proj.shape[1]), F32),
        compiler_params=pltpu.CompilerParams(vmem_limit_bytes=24 * 1024 * 1024),
        cost_estimate=pl.CostEstimate(flops=1, bytes_accessed=1, transcendentals=0),
        name="project_out",
    )(*parts, value_up, out_proj)


def take(stack, index, axis=0):
    return lax.dynamic_index_in_dim(stack, index, axis, keepdims=False)


def tie(*values):
    leaves, tree = jax.tree.flatten(values)
    arrays = [i for i, leaf in enumerate(leaves) if getattr(leaf, "ndim", 0)]
    for i, leaf in zip(arrays, lax.optimization_barrier([leaves[i] for i in arrays])):
        leaves[i] = leaf
    return jax.tree.unflatten(tree, leaves)


def turn_query_kernel(query_width, latent_width, sums_ref, cos_ref, sin_ref, out_ref):
    sums = sums_ref[0]
    for k in range(1, sums_ref.shape[0]):
        sums = sums + sums_ref[k]
    at = query_width + latent_width
    sums = sums * lax.rsqrt(sums[:, at : at + 1] / D + 1e-05)
    cosine, sines = cos_ref[...], sin_ref[...]
    for h in range(query_width // HD):
        one = sums[:, h * HD : (h + 1) * HD]
        one = one * cosine + pltpu.roll(one, HD // 2, 1) * sines
        out_ref[:, h * HD : (h + 1) * HD] = one.astype(BF)
    out_ref[:, query_width:at] = sums[:, query_width:at].astype(BF)


def turn_query(sums, cosine, sines, query_width, latent_width):
    return pl.pallas_call(
        functools.partial(turn_query_kernel, query_width, latent_width),
        out_shape=jax.ShapeDtypeStruct((sums.shape[1], query_width + latent_width), BF),
        compiler_params=pltpu.CompilerParams(vmem_limit_bytes=4 * 1024 * 1024),
        name="turn_query",
    )(sums, cosine, sines)


def pick_kernel(ids_ref, table_ref, weight_ref, keep_ref, send_ref, weight_out, buf, sems, weight_sem):
    bring = pltpu.make_async_copy(weight_ref, weight_out, weight_sem)
    bring.start()
    side = lax.axis_index("side")
    rows = table_ref.shape[0]
    requests, steps = ids_ref.shape
    count = requests * steps
    places = []
    for i in range(count):
        place = ids_ref[i // steps, i % steps] - side * rows
        inside = jnp.logical_and(place >= 0, place < rows)
        place = jnp.where(inside, place, 0)
        start = pl.multiple_of(lax.div(place, FRESH) * FRESH, FRESH)
        pltpu.make_async_copy(table_ref.at[pl.ds(start, FRESH), :], buf.at[i], sems.at[i]).start()
        places.append(jnp.where(inside, place - start, FRESH))
    row = lax.broadcasted_iota(jnp.int32, buf.shape[1:], 0)
    for half in range(2):
        picked = []
        for i in range(half * count // 2, (half + 1) * count // 2):
            pltpu.make_async_copy(table_ref.at[pl.ds(0, FRESH), :], buf.at[i], sems.at[i]).wait()
            one = jnp.where(row == places[i], buf[i].astype(F32), 0.0)
            picked.append(jnp.sum(one, axis=0, keepdims=True))
        picked = jnp.concatenate(picked, axis=0).astype(BF)

        @pl.when(side == half)
        def _():
            keep_ref[...] = picked

        @pl.when(side != half)
        def _():
            send_ref[...] = picked

    bring.wait()


def pick(ids, table, weight):
    width = table.shape[1]
    half = jax.ShapeDtypeStruct((ids.size // 2, width), BF)
    return pl.pallas_call(
        pick_kernel,
        out_shape=(half, half, pltpu.VMEM(weight.shape, weight.dtype)),
        in_specs=[
            pl.BlockSpec(memory_space=pltpu.SMEM),
            pl.BlockSpec(memory_space=pl.ANY),
            pl.BlockSpec(memory_space=pl.ANY),
        ],
        out_specs=[
            pl.BlockSpec(memory_space=pltpu.VMEM),
            pl.BlockSpec(memory_space=pltpu.VMEM),
            pl.BlockSpec(memory_space=pl.ANY),
        ],
        scratch_shapes=[
            pltpu.VMEM((ids.size, FRESH, width), BF),
            pltpu.SemaphoreType.DMA((ids.size,)),
            pltpu.SemaphoreType.DMA,
        ],
        compiler_params=pltpu.CompilerParams(vmem_limit_bytes=12 * 1024 * 1024),
        name="pick",
    )(ids, table, weight)


def new_sums_kernel(blocks, one_ref, other_ref, query_ref, down_ref, keep_ref, send_ref):
    core = lax.rem(lax.axis_index("seq"), 2)
    rows = one_ref[...] + other_ref[...]
    widened = rows.astype(F32)
    squares = jnp.sum(widened * widened, axis=1, keepdims=True)
    latents = jnp.dot(rows, down_ref[...], preferred_element_type=F32)
    query_width = query_ref.shape[1] // blocks
    latent_width = down_ref.shape[1] // blocks
    rest = 128 - latent_width
    for k in range(blocks):
        part = slice(k * query_width, (k + 1) * query_width)
        query = jnp.dot(rows, query_ref[:, part], preferred_element_type=F32)
        tail = jnp.concatenate(
            [
                latents[:, k * latent_width : (k + 1) * latent_width],
                jnp.broadcast_to(squares, (rows.shape[0], rest)),
            ],
            axis=1,
        )
        for same, ref in ((True, keep_ref), (False, send_ref)):

            @pl.when((core == k % 2) == same)
            def _(ref=ref, query=query, tail=tail):
                ref[k // 2, :, :query_width] = query
                ref[k // 2, :, query_width:] = tail


def new_sums(blocks, one, other, query_proj, down_proj):
    width = query_proj.shape[1] // blocks + 128
    half = jax.ShapeDtypeStruct((blocks // 2, one.shape[0], width), F32)
    return pl.pallas_call(
        functools.partial(new_sums_kernel, blocks),
        out_shape=(half, half),
        compiler_params=pltpu.CompilerParams(vmem_limit_bytes=20 * 1024 * 1024),
        name="new_sums",
    )(one, other, query_proj, down_proj)


def arrange_kernel(query_width, *refs):
    refs, (query_ref, fresh_ref) = refs[:-2], refs[-2:]
    grid = Grid()
    heads, rows, width = refs[0].shape
    requests = query_ref.shape[0]
    steps = rows // requests
    cut = width // 2
    each = query_width // HD
    latent_width = cut - query_width
    fresh_ref[...] = jnp.zeros_like(fresh_ref)
    for dy, ref in enumerate(refs):
        y = lax.rem(grid.y + grid.ys - dy, grid.ys)
        for dz in range(heads):
            pair = y * heads + lax.rem(grid.z + heads - dz, heads)
            parts = 2 * each
            first = pair * parts
            g = lax.div(first, HQ // KVH)
            place = lax.rem(first, HQ // KVH) * steps
            for r in range(requests):
                own = []
                for h in range(parts):
                    at = h // each * cut + h % each * HD
                    own.append(ref[dz, r * steps : (r + 1) * steps, at : at + HD])
                start = pl.multiple_of(place, parts * steps)
                query_ref[r, g, pl.ds(start, parts * steps), :] = jnp.concatenate(own, axis=0)
            latents = [
                ref[dz, :, core * cut + query_width : (core + 1) * cut] for core in range(2)
            ]
            latents = jnp.concatenate(latents, axis=1)
            for r in range(requests):
                fresh_ref[r, pair, :steps, :] = latents[r * steps : (r + 1) * steps, :]


def arrange(by_y, requests, query_width):
    heads, rows, width = by_y[0].shape
    steps = rows // requests
    latents = width - 2 * query_width
    return pl.pallas_call(
        functools.partial(arrange_kernel, query_width),
        out_shape=(
            jax.ShapeDtypeStruct((requests, KVH, HQ // KVH * steps, HD), BF),
            jax.ShapeDtypeStruct((requests, len(by_y) * heads, FRESH, latents), BF),
        ),
        compiler_params=pltpu.CompilerParams(vmem_limit_bytes=8 * 1024 * 1024),
        name="arrange",
    )(*by_y)


def in_a_box(holds, step, *values):
    shapes = jax.eval_shape(step, *values)

    def otherwise(*_):
        return jax.tree.map(lambda one: jnp.zeros(one.shape, one.dtype), shapes)

    return lax.cond(holds, step, otherwise, *values)


def in_order(parts, mine):
    count = len(parts)
    if count == 2:
        swap = mine == 0
        return jnp.stack([jnp.where(swap, parts[0], parts[1]), jnp.where(swap, parts[1], parts[0])])
    twice = jnp.stack(parts[::-1] * 2)
    return lax.dynamic_slice_in_dim(twice, count - 1 - mine, count, 0)


def local(
    cached_hidden,
    page_order,
    lengths,
    new_ids,
    embedding,
    query_proj,
    down_proj,
    key_up,
    value_up,
    out_proj,
):
    grid = Grid()
    side, y, c, z = grid.side, grid.y, grid.c, grid.z
    ys, heads = grid.ys, grid.heads
    requests, span, width = cached_hidden.shape
    tokens, steps = new_ids.shape
    rows = requests * steps
    depth = down_proj.shape[0]
    hidden = cached_hidden.reshape(requests * span, width)
    hidden = pltpu.with_memory_space_constraint(hidden, pltpu.HBM)
    holds = new_ids[0, 0] >= 0

    def on_cores(*segments):
        return [
            [(rows, dy, dc, dz, base, step) for rows, dy, dz, base, step in segments]
            for dc in range(2)
        ]

    def both(piece, *segments):
        here, there = on_cores(*segments)
        return [(piece, here), (grid.send(piece, core=1), there)]

    def swapped(pieces):
        pairs = []
        for i, piece in enumerate(pieces):
            if i >= 2:
                piece, _ = tie(piece, pairs[i - 2][1])
            pairs.append((piece, grid.send(piece, core=1)))
        return pairs

    def add_pairs(pairs, places, latent):
        batch = []
        for pair, segments in zip(pairs, places):
            batch += list(zip(pair, on_cores(*segments)))
        return add_latents(hidden, depth, batch, latent)

    def project_shared(own, between):
        b = depth // 4

        def edge(piece):
            return piece, b, 0, 2 * b

        embed, over_y, over_head, spread, over_all, lay_out = between
        r0 = first_piece(own, key_up, b)
        r1 = grid.send(r0, head=1)
        y0 = grid.send(r0, y=1)

        extra = in_a_box(holds, lambda ids: over_y(embed(ids)), tie(new_ids, r0)[0])
        r1, y0, extra = tie(r1, y0, extra)

        other = (3 * b, -3 * b)
        at_own = [(4 * b, 0, 0, 0, 0)]
        at_r = [None] + [[(3 * b, 0, k, 0, b)] for k in range(1, heads)]
        at_y = [[(3 * b, 1, k, 0, b)] for k in range(3)] + [[(2 * b, 1, 3, 0, 2 * b)]]
        at_x = [
            None,
            [(b, 0, 1, *other), (b, 1, 0, *other)],
            [(b, 0, 2, *other), (b, 1, 1, *other)],
            [(b, 0, 3, *other), (b, 1, 2, *other)],
            [(2 * b, 1, 3, 2 * b, -2 * b)],
        ]

        r2 = grid.send(r1, head=1)
        y1 = grid.send(r1, y=1)
        (edges,) = assemble([edge(r1), edge(y0)])
        x1 = grid.send(edges, side=1)

        def first_latents(*pieces):
            latent = add_pairs(swapped(pieces), [at_own, at_r[1], at_y[0]], None)
            return latent, r0[3 * b :], r1[3 * b :]

        latent, up0, up1 = in_a_box(holds, first_latents, tie(own, edges)[0], r1, y0)
        tables = make_tables(*tie(lengths, page_order, r1)[:2])
        r2, y1, x1, latent, tables, extra = tie(r2, y1, x1, latent, tables, extra)

        r3 = grid.send(r2, head=1)
        y2 = grid.send(r2, y=1)
        (edges,) = assemble([edge(r2), edge(y1)])
        x2 = grid.send(edges, side=1)

        def second_latents(pieces, latent, extra):
            extra = over_head(extra)
            latent = add_pairs(swapped(pieces), [at_r[2], at_y[1], at_x[1]], latent)
            return latent, extra, pieces[0][3 * b :]

        latent, extra, up2 = in_a_box(holds, second_latents, (r2, y1, x1), latent, extra)
        r3, y2, x2, latent, extra = tie(r3, y2, x2, latent, extra)

        last, edges = assemble([(r3, 2 * b, 0, b)], [edge(r3), edge(y2)])
        y3 = grid.send(last, y=1)
        x3 = grid.send(edges, side=1)
        tables, turns = tables
        extra, last = tie(extra, last)

        def third_latents(pieces, latent, extra, *turns):
            pairs = swapped(pieces)
            extra = spread(extra, *turns, pairs)
            return add_pairs(pairs, [at_r[3], at_y[2]], latent), extra, pieces[0][3 * b :]

        latent, extra, up3 = in_a_box(holds, third_latents, (r3, y2), latent, extra, *turns)
        x2, x3, y3, latent, extra = tie(x2, x3, y3, latent, extra)

        x4 = grid.send(y3, side=1)

        def fourth_latents(pieces, latent, extra):
            extra = over_all(extra)
            latent = add_pairs(swapped(pieces), [at_x[2], at_y[3], at_x[3]], latent)
            return latent, lay_out(extra)

        latent, extra = in_a_box(holds, fourth_latents, (x2, y3, x3), latent, extra)
        x4, latent, extra = tie(x4, latent, extra)
        batch = list(zip((x4, grid.send(x4, core=1)), on_cores(*at_x[4])))
        return batch, latent, (extra, ([up0, up1, up2, up3], 0), tables)

    def project_plain(own, between):
        latent = None
        ring = own
        for k in range(heads):
            if k:
                ring = grid.send(ring, head=1)
            if k:
                latent = add_latents(hidden, depth, batch, latent)
            batch = both(ring, (depth, 0, k, 0, 0))
            for dy in range(1, ys):
                latent = add_latents(hidden, depth, batch, latent)
                batch = both(grid.send(ring, y=dy), (depth, dy, k, 0, 0))
        tables, turns = make_tables(lengths, page_order)
        embed, over_y, over_head, spread, over_all, lay_out = between
        extra = spread(over_head(over_y(embed(new_ids))), *turns)
        extra = lay_out(over_all(extra))
        ups = [pack_up(key_up)]
        ups += [grid.send(ups[0], head=k) for k in range(1, heads)]
        return batch, latent, (extra, (ups, 0), tables)

    blocks = 2 * ys * heads
    query_width = query_proj.shape[1] // blocks
    latent_width = down_proj.shape[1] // blocks
    cut = query_width + latent_width

    def embed(ids):
        keep, rest, weight = pick(ids, embedding, query_proj)
        keep, rest = new_sums(blocks, keep, grid.send(rest, side=1), weight, down_proj)
        packed = keep + grid.send(rest, core=1)
        return packed.reshape(ys, heads, rows, -1)

    def reduce_over_y(packed):
        kept = take(packed, y)
        for dy in range(1, ys):
            kept = kept + grid.send(take(packed, (y + dy) % ys), y=dy)
        return kept

    def reduce_over_head(kept):
        return lax.all_to_all(kept, "head", 0, 0)

    def spread_query(mine, cosine, sines, after=()):
        block = turn_query(mine, cosine, sines, query_width, latent_width)
        pair = in_order([block, grid.send(block, core=1)], c)
        pair, _ = tie(jnp.concatenate([pair[0], pair[1]], axis=-1), after)
        return jnp.stack([pair] + [grid.send(pair, head=k) for k in range(1, heads)])

    def spread_over_y(by_head):
        return [by_head] + [grid.send(by_head, y=k) for k in range(1, ys)]

    def lay_out(by_y):
        return arrange(by_y, requests, query_width)

    def make_tables(lengths, page_order):
        pages = page_order.shape[1]
        logical = jnp.arange(pages, dtype=jnp.int32)
        page_of = jnp.sum(
            jnp.where(page_order[:, :, None] == logical[None, None, :], logical[None, :, None], 0), axis=1
        )
        start = ((y * 2 + c) * heads + z) * span
        positions = (
            start + page_of[:, :, None] * PAGE + jnp.arange(PAGE, dtype=jnp.int32)[None, None, :]
        ).reshape(requests, span)
        new_rows = jnp.arange(FRESH, dtype=jnp.int32)
        row_positions = jnp.concatenate(
            [positions, lengths[:, None] + jnp.minimum(new_rows, steps - 1)[None, :]], axis=1
        )
        cosine, sines = sincos(row_positions)
        lanes = max(128, HQ // KVH * steps)
        step_of = jnp.arange(lanes, dtype=jnp.int32) % steps
        holds_new = (y == 0) & (c == 0) & (z == 0)
        new_seen = (new_rows[:, None] <= step_of[None, :]) & holds_new
        live = jnp.concatenate(
            [
                jnp.broadcast_to((positions < lengths[:, None])[:, :, None], (requests, span, lanes)),
                jnp.broadcast_to(new_seen[None], (requests, FRESH, lanes)),
            ],
            axis=1,
        ).astype(F32)
        fresh_positions = lengths[:, None] + jnp.arange(steps, dtype=jnp.int32)[None, :]
        return (cosine, sines, live), sincos(fresh_positions.reshape(-1))

    between = [embed, reduce_over_y, reduce_over_head, spread_query, spread_over_y, lay_out]
    shared = ys == 2 and heads == 4 and grid.sides == 2 and depth % 512 == 0
    batch, latent, extra = (project_shared if shared else project_plain)(down_proj, between)
    (queries, fresh), (ups, up_row), (cosine, sines, live) = extra
    weight = pltpu.with_memory_space_constraint(out_proj, pltpu.HBM)
    states, weight = finish(
        span, hidden, depth, batch, latent, fresh, cosine, sines, live, queries, ups,
        up_row, weight, heads,
    )
    parts = [take(states, z)]
    for dz in range(1, heads):
        parts.append(grid.send(take(states, (z + dz) % heads), head=dz))
    state = join_parts(parts)
    states = [state]
    for dy in range(ys):
        for dc in range(2):
            if dy or dc:
                states.append(grid.send(state, y=dy, core=dc))
    partial_out = project_out(states, value_up, weight, requests, steps)
    sent = partial_out.astype(BF)
    attended = partial_out
    for dz in range(1, heads):
        attended = attended + grid.send(sent, head=dz).astype(F32)
    return attended.astype(BF).reshape(requests, steps, -1)


def solution(mesh):
    return jax.shard_map(
        local,
        mesh=mesh,
        in_specs=(
            P("side", ("seq", "head"), None),
            P("side", ("seq", "head")),
            P("side"),
            P(),
            P("side", ("seq", "head")),
            P(("seq", "head"), None),
            P(("seq", "head"), None),
            P("head", None, None),
            P("head", None, None),
            P("head", "seq"),
        ),
        out_specs=P("side", None, "seq"),
        check_vma=False,
    )
```

```python
import functools
import math

import jax
import jax.numpy as jnp
from jax import lax
from jax.experimental import pallas as pl
from jax.experimental.pallas import tpu as pltpu
from jax.sharding import PartitionSpec as P

D = 8192
HQ = 64
KVH = 8
HD = 128
RANK = 64
PAGE = 16
FRESH = 16

AXES = ("side", "seq", "head")
rope_base = 500000.0
masked_score = -1e30
BF = jnp.bfloat16
F32 = jnp.float32


def sincos(positions):
    half = HD // 2
    frequency = 1.0 / rope_base ** (jnp.arange(half, dtype=F32) * 2.0 / HD)
    angles = positions.astype(F32)[..., None] * frequency
    cosine, sines = jnp.cos(angles), jnp.sin(angles)
    return (
        jnp.concatenate([cosine, cosine], axis=-1),
        jnp.concatenate([-sines, sines], axis=-1),
    )


class Grid:
    def __init__(self):
        self.sides, self.seqs, self.heads = (lax.axis_size(a) for a in AXES)
        self.ys = self.seqs // 2
        self.side, seq, self.z = (lax.axis_index(a) for a in AXES)
        self.y, self.c = lax.div(seq, 2), lax.rem(seq, 2)

    def send(self, value, side=0, y=0, core=0, head=0):
        pairs = []
        for a in range(self.sides):
            for b in range(self.ys):
                for c in range(2):
                    for d in range(self.heads):
                        to = (
                            (a + side) % self.sides,
                            (b + y) % self.ys,
                            (c + core) % 2,
                            (d + head) % self.heads,
                        )
                        pairs.append((self.flat(a, b, c, d), self.flat(*to)))
        return lax.ppermute(value, AXES, pairs)

    def place(self, dy, dc, dz):
        seq = lax.rem(self.y + self.ys - dy, self.ys) * 2 + (1 - self.c if dc else self.c)
        return seq * self.heads + lax.rem(self.z + self.heads - dz, self.heads)

    def flat(self, a, b, c, d):
        return (a * self.seqs + b * 2 + c) * self.heads + d


def accumulate(
    counts, segments, depth, hidden_ref, pieces, before_ref, hidden_buf, piece_buf, total, sems, store=None
):
    grid = Grid()
    rows = hidden_ref.shape[0]
    if before_ref is not None:
        load = pltpu.make_async_copy(before_ref, total, sems.at[len(segments) + len(pieces)])
    waits = []
    at = 0
    for i, count in enumerate(counts):
        copies = [
            pltpu.make_async_copy(
                pieces[i].at[pl.ds(0, count), :],
                piece_buf.at[pl.ds(at, count), :],
                sems.at[len(segments) + i],
            )
        ]
        inside = 0
        for k, (owner, extent, dy, dc, dz, base, step) in enumerate(segments):
            if owner == i:
                source = grid.place(dy, dc, dz) * depth + base + step * grid.side
                source = pl.multiple_of(source, 128)
                copies.append(
                    pltpu.make_async_copy(
                        hidden_ref.at[:, pl.ds(source, extent)],
                        hidden_buf.at[:, pl.ds(at + inside, extent)],
                        sems.at[k],
                    )
                )
                inside += extent
        for copy in copies:
            copy.start()
        if before_ref is not None and i == 1:
            load.start()
        waits.append((copies, at, count))
        at += count
    pairs = [waits[i : i + 2] for i in range(0, len(waits), 2)]
    for k, pair in enumerate(pairs):
        for copies, _, _ in pair:
            for copy in copies:
                copy.wait()
        first = pair[0][1]
        span = sum(count for _, _, count in pair)
        last = k == len(pairs) - 1
        tile = rows // 4 if last and store else rows
        for m in range(rows // tile):
            part = slice(m * tile, (m + 1) * tile)
            term = jnp.dot(
                hidden_buf[part, first : first + span],
                piece_buf[first : first + span, :],
                preferred_element_type=F32,
            )
            if k == 0 and m == 0 and before_ref is not None:
                load.wait()
            total[part, :] = total[part, :] + term if k or before_ref is not None else term
            if last and store:
                store(m, tile)


def latent_kernel(counts, segments, depth, has_total, hidden_ref, *refs):
    pieces, refs = refs[: len(counts)], refs[len(counts) :]
    before_ref = None
    if has_total:
        before_ref, refs = refs[0], refs[1:]
    out_ref, hidden_buf, piece_buf, total, sems, out_sems = refs
    stores = []

    def store(m, tile):
        rows = pl.ds(m * tile, tile)
        copy = pltpu.make_async_copy(total.at[rows, :], out_ref.at[rows, :], out_sems.at[m])
        copy.start()
        stores.append(copy)

    accumulate(
        counts, segments, depth, hidden_ref, pieces, before_ref, hidden_buf, piece_buf, total, sems, store
    )
    for copy in stores:
        copy.wait()


def add_latents(hidden, depth, batch, total=None):
    pieces = [piece for piece, _ in batch]
    counts = [sum(part[0] for part in parts) for _, parts in batch]
    segments = [(i, *part) for i, (_, parts) in enumerate(batch) for part in parts]
    deep, columns = sum(counts), pieces[0].shape[1]
    rows = hidden.shape[0]
    operands = [hidden, *pieces]
    if total is not None:
        operands.append(total)
    return pl.pallas_call(
        functools.partial(latent_kernel, counts, segments, depth, total is not None),
        out_shape=jax.ShapeDtypeStruct((rows, columns), F32),
        in_specs=[pl.BlockSpec(memory_space=pl.ANY)] * len(operands),
        out_specs=pl.BlockSpec(memory_space=pl.ANY),
        scratch_shapes=[
            pltpu.VMEM((rows, deep), BF),
            pltpu.VMEM((deep, columns), BF),
            pltpu.VMEM((rows, columns), F32),
            pltpu.SemaphoreType.DMA((len(segments) + len(pieces) + 1,)),
            pltpu.SemaphoreType.DMA((4,)),
        ],
        compiler_params=pltpu.CompilerParams(vmem_limit_bytes=28 * 1024 * 1024),
        cost_estimate=pl.CostEstimate(
            flops=2 * rows * deep * columns,
            bytes_accessed=2 * deep * (rows + columns) + 8 * rows * columns,
            transcendentals=0,
        ),
        name="latents",
    )(*operands)


def first_piece_kernel(rows, own_ref, up_ref, out_ref, sems):
    side = lax.axis_index("side")
    groups = up_ref.shape[0]
    each = RANK // FRESH
    start = pl.multiple_of(rows * side, 16)
    copies = [
        pltpu.make_async_copy(
            own_ref.at[pl.ds(start, 3 * rows), :], out_ref.at[pl.ds(0, 3 * rows), :], sems.at[0]
        )
    ]
    for k in range(groups * each):
        copies.append(
            pltpu.make_async_copy(
                up_ref.at[k // each, pl.ds(k % each * FRESH, FRESH), :],
                out_ref.at[pl.ds(3 * rows, FRESH), pl.ds(k * HD, HD)],
                sems.at[1 + k],
            )
        )
    for copy in copies:
        copy.start()
    for copy in copies:
        copy.wait()


def first_piece(own, key_up, rows):
    count = key_up.shape[0] * RANK // FRESH
    return pl.pallas_call(
        functools.partial(first_piece_kernel, rows),
        out_shape=jax.ShapeDtypeStruct((3 * rows + FRESH, own.shape[1]), own.dtype),
        in_specs=[pl.BlockSpec(memory_space=pl.ANY)] * 2,
        out_specs=pl.BlockSpec(memory_space=pltpu.VMEM),
        scratch_shapes=[pltpu.SemaphoreType.DMA((1 + count,))],
        compiler_params=pltpu.CompilerParams(vmem_limit_bytes=8 * 1024 * 1024),
        cost_estimate=pl.CostEstimate(flops=1, bytes_accessed=1, transcendentals=0),
        name="first_piece",
    )(own, key_up)


def assemble_kernel(layout, *refs):
    ins, outs, sems = refs[: len(layout)], refs[len(layout) : -1], refs[-1]
    side = lax.axis_index("side")
    copies = []
    for k, (o, at, count, base, step) in enumerate(layout):
        start = pl.multiple_of(base + step * side, 16)
        copies.append(
            pltpu.make_async_copy(
                ins[k].at[pl.ds(start, count), :], outs[o].at[pl.ds(at, count), :], sems.at[k]
            )
        )
        copies[-1].start()
    for copy in copies:
        copy.wait()


def assemble(*arrays):
    layout, sources, shapes = [], [], []
    for o, parts in enumerate(arrays):
        at = 0
        for source, count, base, step in parts:
            layout.append((o, at, count, base, step))
            sources.append(source)
            at += count
        shapes.append(jax.ShapeDtypeStruct((at, source.shape[1]), source.dtype))
    return pl.pallas_call(
        functools.partial(assemble_kernel, layout),
        out_shape=shapes,
        in_specs=[pl.BlockSpec(memory_space=pl.ANY)] * len(sources),
        out_specs=[pl.BlockSpec(memory_space=pltpu.VMEM)] * len(shapes),
        scratch_shapes=[pltpu.SemaphoreType.DMA((len(layout),))],
        compiler_params=pltpu.CompilerParams(vmem_limit_bytes=8 * 1024 * 1024),
        cost_estimate=pl.CostEstimate(flops=1, bytes_accessed=1, transcendentals=0),
        name="assemble",
    )(*sources)


def in_three(value):
    high = value.astype(BF).astype(F32)
    middle = (value - high).astype(BF).astype(F32)
    return high, middle, value - high - middle


def pack_up(key_up):
    groups = key_up.shape[0]
    parts = key_up.reshape(groups, RANK // FRESH, FRESH, HD).transpose(2, 0, 1, 3)
    return parts.reshape(FRESH, -1)


def unpack_up(up_ref, g):
    each = up_ref.shape[2] // (RANK // FRESH * HD)
    at = g % each * (RANK // FRESH)
    parts = [up_ref[g // each, :, (at + i) * HD : (at + i + 1) * HD] for i in range(RANK // FRESH)]
    return jnp.concatenate(parts, axis=0)


def attend_part(scale, span, lat_ref, fresh_ref, cos_ref, sin_ref, live_ref, query_ref, up_ref, out_ref):
    requests, groups, lanes, _ = query_ref.shape
    blocks = out_ref.shape[0]
    each = groups // blocks
    peaks, totals, summed = [], [], []
    ups = [unpack_up(up_ref, g) for g in range(groups)]
    for r in range(requests):
        latent = jnp.concatenate(
            [
                lat_ref[r * span : (r + 1) * span, :].astype(BF),
                jnp.concatenate([fresh_ref[r, p] for p in range(fresh_ref.shape[1])], axis=1),
            ],
            axis=0,
        )
        cosine, sines = cos_ref[r], sin_ref[r]
        columns, values = [], []
        for g in range(groups):
            at = g * 2 * RANK
            key = jnp.dot(latent[:, at : at + RANK], ups[g], preferred_element_type=F32)
            key = (key * cosine + pltpu.roll(key, HD // 2, 1) * sines).astype(BF)
            columns.append(
                lax.dot_general(
                    key, query_ref[r, g], (((1,), (1,)), ((), ())), preferred_element_type=F32
                )
            )
            values.append(latent[:, at + RANK : at + 2 * RANK])
        scores = jnp.concatenate(columns, axis=1) * scale
        live = live_ref[r] > 0
        live = jnp.concatenate([live] * (scores.shape[1] // live.shape[1]), axis=1)
        scores = jnp.where(live, scores, masked_score)
        peak = jnp.max(scores, axis=0, keepdims=True)
        weights = jnp.where(live, jnp.exp(scores - peak), 0.0)
        peaks.append(peak)
        totals.append(jnp.sum(weights, axis=0, keepdims=True))
        summed.append(
            lax.dot_general(
                jnp.concatenate(values, axis=1),
                weights.astype(BF),
                (((0,), (0,)), ((), ())),
                preferred_element_type=F32,
            )
        )
    for b in range(blocks):
        stats = []
        for i in range(each):
            g = b * each + i
            cut = slice(g * lanes, (g + 1) * lanes)
            out_ref[b, i * RANK : (i + 1) * RANK, :] = jnp.concatenate(
                [s[g * RANK : (g + 1) * RANK, cut] for s in summed], axis=1
            ).astype(BF)
            stats += in_three(jnp.concatenate([p[:, cut] for p in peaks], axis=1))
            stats += in_three(jnp.concatenate([t[:, cut] for t in totals], axis=1))
        stats += [jnp.zeros_like(stats[0])] * (16 - len(stats))
        out_ref[b, each * RANK :, :] = jnp.concatenate(stats, axis=0).astype(BF)


def lay_tables(span, steps, start, order_ref, length_ref, small_cos, small_sin, cos_ref, sin_ref, live_ref):
    requests, rows, lanes = cos_ref.shape
    pages = order_ref.shape[1]
    padded = -(-pages // 16) * 16
    inner_cos, inner_sin = small_cos[padded : padded + PAGE, :], small_sin[padded : padded + PAGE, :]
    inner = lax.broadcasted_iota(jnp.int32, (PAGE, lanes), 0)
    grid = Grid()
    first = grid.place(0, 0, 0) == 0
    column_step = lax.rem(lax.broadcasted_iota(jnp.int32, (FRESH, lanes), 1), steps)
    new_row = lax.broadcasted_iota(jnp.int32, (FRESH, lanes), 0)
    seen = jnp.where(jnp.logical_and(new_row <= column_step, first), 1.0, 0.0)
    for j in range(pages):
        page_cos, page_sin = small_cos[j : j + 1, :], small_sin[j : j + 1, :]
        cosine = page_cos * inner_cos - page_sin * inner_sin
        sines = page_sin * inner_cos + page_cos * inner_sin
        for r in range(requests):
            at = pl.multiple_of(order_ref[r, j] * PAGE, PAGE)
            cos_ref[r, pl.ds(at, PAGE), :] = cosine
            sin_ref[r, pl.ds(at, PAGE), :] = sines
            position = start + j * PAGE + inner
            live_ref[r, pl.ds(at, PAGE), :] = jnp.where(position < length_ref[r], 1.0, 0.0)
    fill = jnp.zeros((FRESH - steps, lanes), F32)
    new = padded + PAGE
    for r in range(requests):
        own = slice(new + r * steps, new + (r + 1) * steps)
        cos_ref[r, span:, :] = jnp.concatenate([small_cos[own, :], fill], axis=0)
        sin_ref[r, span:, :] = jnp.concatenate([small_sin[own, :], fill], axis=0)
        live_ref[r, span:, :] = seen


def finish_kernel(counts, segments, depth, scale, span, up_row, steps, order_ref, length_ref, *refs):
    small_cos, small_sin, hidden_ref, refs = refs[0], refs[1], refs[2], refs[3:]
    pieces, refs = refs[: len(counts)], refs[len(counts) :]
    heads = lax.axis_size("head")
    before_ref, tables, ups, weight_ref = refs[0], refs[1:3], refs[3 : 3 + heads], refs[3 + heads]
    out_ref, weight_out, hidden_buf, piece_buf, total, *refs = refs[4 + heads :]
    held, (cos_ref, sin_ref, live_ref, up_buf, sems, table_sems, weight_sem) = refs[:2], refs[2:]
    loads = [
        pltpu.make_async_copy(table, buf, table_sems.at[i])
        for i, (table, buf) in enumerate(zip(tables, held))
    ]
    z = lax.axis_index("head")
    for k, up in enumerate(ups):
        place = lax.rem(z + heads - k, heads)
        loads.append(
            pltpu.make_async_copy(
                up.at[pl.ds(up_row, FRESH), :], up_buf.at[place], table_sems.at[len(tables) + k]
            )
        )
    for load in loads:
        load.start()
    grid = Grid()
    start = grid.place(0, 0, 0) * span
    lay_tables(
        span, steps, start, order_ref, length_ref, small_cos, small_sin, cos_ref, sin_ref, live_ref
    )
    accumulate(counts, segments, depth, hidden_ref, pieces, before_ref, hidden_buf, piece_buf, total, sems)
    for load in loads:
        load.wait()
    bring = pltpu.make_async_copy(weight_ref, weight_out, weight_sem)
    bring.start()
    fresh, queries = held
    attend_part(scale, span, total, fresh, cos_ref, sin_ref, live_ref, queries, up_buf, out_ref)
    bring.wait()


def finish(
    span, hidden, depth, batch, total, fresh, cosine, sines, queries, ups, up_row, weight, blocks,
    page_order, lengths, steps,
):
    pieces = [piece for piece, _ in batch]
    counts = [sum(part[0] for part in parts) for _, parts in batch]
    segments = [(i, *part) for i, (_, parts) in enumerate(batch) for part in parts]
    deep, columns = sum(counts), pieces[0].shape[1]
    rows = hidden.shape[0]
    requests, groups, lanes, _ = queries.shape
    tables = (fresh, queries)
    wide = (requests, span + FRESH, HD)
    total = pltpu.with_memory_space_constraint(total, pltpu.VMEM)
    operands = [page_order, lengths, cosine, sines, hidden, *pieces, total, *tables, *ups, weight]
    far = [pl.BlockSpec(memory_space=pl.ANY)] * (len(operands) - 4)
    state_rows = groups // blocks * RANK + 16
    return pl.pallas_call(
        functools.partial(
            finish_kernel, counts, segments, depth, 1.0 / math.sqrt(HD), span, up_row, steps
        ),
        out_shape=(
            jax.ShapeDtypeStruct((blocks, state_rows, requests * lanes), BF),
            pltpu.VMEM(weight.shape, weight.dtype),
        ),
        in_specs=[pl.BlockSpec(memory_space=pltpu.SMEM)] * 2
        + [pl.BlockSpec(memory_space=pltpu.VMEM)] * 2
        + far,
        out_specs=(pl.BlockSpec(memory_space=pltpu.VMEM), pl.BlockSpec(memory_space=pl.ANY)),
        scratch_shapes=[
            pltpu.VMEM((rows, deep), BF),
            pltpu.VMEM((deep, columns), BF),
            pltpu.VMEM((rows, columns), F32),
        ]
        + [pltpu.VMEM(table.shape, table.dtype) for table in tables]
        + [pltpu.VMEM(wide, F32)] * 3
        + [
            pltpu.VMEM((len(ups), FRESH, ups[0].shape[1]), BF),
            pltpu.SemaphoreType.DMA((len(segments) + len(pieces) + 1,)),
            pltpu.SemaphoreType.DMA((len(tables) + len(ups),)),
            pltpu.SemaphoreType.DMA,
        ],
        compiler_params=pltpu.CompilerParams(vmem_limit_bytes=18 * 1024 * 1024),
        cost_estimate=pl.CostEstimate(flops=1, bytes_accessed=1, transcendentals=0),
        name="finish",
    )(*operands)


def join(states):
    peak = functools.reduce(jnp.maximum, [p for p, _, _ in states])
    total, summed = 0.0, 0.0
    for p, t, s in states:
        weight = jnp.exp(p - peak)
        total = total + t * weight
        summed = summed + s * weight
    return peak, total, summed


def pack(states, out_ref):
    each = len(states)
    stats = []
    for i, (peak, total, summed) in enumerate(states):
        out_ref[i * RANK : (i + 1) * RANK, :] = summed.astype(BF)
        stats += [*in_three(peak), *in_three(total)]
    stats += [jnp.zeros_like(stats[0])] * (16 - len(stats))
    out_ref[each * RANK :, :] = jnp.concatenate(stats, axis=0).astype(BF)


def unpack(ref, each):
    stats = ref[each * RANK :, :].astype(F32)
    states = []
    for i in range(each):
        three = [stats[at : at + 1] for at in range(6 * i, 6 * i + 6)]
        peak, total = three[0] + three[1] + three[2], three[3] + three[4] + three[5]
        states.append((peak, total, ref[i * RANK : (i + 1) * RANK, :].astype(F32)))
    return states


def join_parts_kernel(each, *refs):
    refs, out_ref = refs[:-1], refs[-1]
    parts = [unpack(ref, each) for ref in refs]
    pack([join([part[i] for part in parts]) for i in range(each)], out_ref)


def join_parts(parts):
    return pl.pallas_call(
        functools.partial(join_parts_kernel, (parts[0].shape[0] - 16) // RANK),
        out_shape=jax.ShapeDtypeStruct(parts[0].shape, BF),
        compiler_params=pltpu.CompilerParams(vmem_limit_bytes=4 * 1024 * 1024),
        cost_estimate=pl.CostEstimate(flops=1, bytes_accessed=1, transcendentals=0),
        name="join_parts",
    )(*parts)


def project_out_kernel(requests, steps, *refs):
    up_ref, weight_ref, out_ref = refs[-3:]
    each = up_ref.shape[0]
    parts = [unpack(ref, each) for ref in refs[:-3]]
    lanes = refs[0].shape[1]
    rows = requests * steps
    heads = lanes // rows
    old = lax.broadcasted_iota(jnp.int32, (lanes, lanes), 0)
    new = lax.broadcasted_iota(jnp.int32, (lanes, lanes), 1)
    request, rest = old // (heads * steps), old % (heads * steps)
    moved = (rest // steps) * rows + request * steps + rest % steps
    order = jnp.where(moved == new, 1.0, 0.0).astype(BF)
    context = []
    for i in range(each):
        _, total, summed = join([part[i] for part in parts])
        scaled = (summed / total).astype(BF)
        one = lax.dot_general(
            up_ref[i], scaled, (((0,), (0,)), ((), ())), preferred_element_type=F32
        ).astype(BF)
        one = lax.dot_general(
            order, one, (((0,), (1,)), ((), ())), preferred_element_type=F32
        ).astype(BF)
        context += [one[j * rows : (j + 1) * rows, :] for j in range(heads)]
    out_ref[...] = jnp.dot(
        jnp.concatenate(context, axis=1), weight_ref[...], preferred_element_type=F32
    )


def project_out(parts, value_up, out_proj, requests, steps):
    return pl.pallas_call(
        functools.partial(project_out_kernel, requests, steps),
        out_shape=jax.ShapeDtypeStruct((requests * steps, out_proj.shape[1]), F32),
        compiler_params=pltpu.CompilerParams(vmem_limit_bytes=24 * 1024 * 1024),
        cost_estimate=pl.CostEstimate(flops=1, bytes_accessed=1, transcendentals=0),
        name="project_out",
    )(*parts, value_up, out_proj)


def take(stack, index, axis=0):
    return lax.dynamic_index_in_dim(stack, index, axis, keepdims=False)


def tie(*values):
    leaves, tree = jax.tree.flatten(values)
    arrays = [i for i, leaf in enumerate(leaves) if getattr(leaf, "ndim", 0)]
    for i, leaf in zip(arrays, lax.optimization_barrier([leaves[i] for i in arrays])):
        leaves[i] = leaf
    return jax.tree.unflatten(tree, leaves)


def turn_query_kernel(query_width, latent_width, sums_ref, cos_ref, sin_ref, out_ref):
    sums = sums_ref[0]
    for k in range(1, sums_ref.shape[0]):
        sums = sums + sums_ref[k]
    at = query_width + latent_width
    sums = sums * lax.rsqrt(sums[:, at : at + 1] / D + 1e-05)
    own = slice(cos_ref.shape[0] - sums.shape[0], None)
    cosine, sines = cos_ref[own, :], sin_ref[own, :]
    for h in range(query_width // HD):
        one = sums[:, h * HD : (h + 1) * HD]
        one = one * cosine + pltpu.roll(one, HD // 2, 1) * sines
        out_ref[:, h * HD : (h + 1) * HD] = one.astype(BF)
    out_ref[:, query_width:at] = sums[:, query_width:at].astype(BF)


def turn_query(sums, cosine, sines, query_width, latent_width):
    return pl.pallas_call(
        functools.partial(turn_query_kernel, query_width, latent_width),
        out_shape=jax.ShapeDtypeStruct((sums.shape[1], query_width + latent_width), BF),
        compiler_params=pltpu.CompilerParams(vmem_limit_bytes=4 * 1024 * 1024),
        name="turn_query",
    )(sums, cosine, sines)


def pick_kernel(ids_ref, table_ref, keep_ref, send_ref, buf, sems):
    side = lax.axis_index("side")
    rows = table_ref.shape[0]
    requests, steps = ids_ref.shape
    count = requests * steps
    places = []
    for i in range(count):
        place = ids_ref[i // steps, i % steps] - side * rows
        inside = jnp.logical_and(place >= 0, place < rows)
        place = jnp.where(inside, place, 0)
        start = pl.multiple_of(lax.div(place, FRESH) * FRESH, FRESH)
        pltpu.make_async_copy(table_ref.at[pl.ds(start, FRESH), :], buf.at[i], sems.at[i]).start()
        places.append(jnp.where(inside, place - start, FRESH))
    row = lax.broadcasted_iota(jnp.int32, buf.shape[1:], 0)
    for half in range(2):
        picked = []
        for i in range(half * count // 2, (half + 1) * count // 2):
            pltpu.make_async_copy(table_ref.at[pl.ds(0, FRESH), :], buf.at[i], sems.at[i]).wait()
            one = jnp.where(row == places[i], buf[i].astype(F32), 0.0)
            picked.append(jnp.sum(one, axis=0, keepdims=True))
        picked = jnp.concatenate(picked, axis=0).astype(BF)

        @pl.when(side == half)
        def _():
            keep_ref[...] = picked

        @pl.when(side != half)
        def _():
            send_ref[...] = picked


def pick(ids, table):
    width = table.shape[1]
    half = jax.ShapeDtypeStruct((ids.size // 2, width), BF)
    return pl.pallas_call(
        pick_kernel,
        out_shape=(half, half),
        in_specs=[pl.BlockSpec(memory_space=pltpu.SMEM), pl.BlockSpec(memory_space=pl.ANY)],
        scratch_shapes=[
            pltpu.VMEM((ids.size, FRESH, width), BF),
            pltpu.SemaphoreType.DMA((ids.size,)),
        ],
        compiler_params=pltpu.CompilerParams(vmem_limit_bytes=4 * 1024 * 1024),
        name="pick",
    )(ids, table)


def new_sums_kernel(
    blocks, one_ref, other_ref, query_far, down_ref, keep_ref, send_ref, query_ref, sems
):
    wide = query_ref.shape[1] // sems.shape[0]
    copies = []
    for k in range(sems.shape[0]):
        part = pl.ds(k * wide, wide)
        copies.append(
            pltpu.make_async_copy(query_far.at[:, part], query_ref.at[:, part], sems.at[k])
        )
        copies[-1].start()
    core = lax.rem(lax.axis_index("seq"), 2)
    rows = one_ref[...] + other_ref[...]
    widened = rows.astype(F32)
    squares = jnp.sum(widened * widened, axis=1, keepdims=True)
    latents = jnp.dot(rows, down_ref[...], preferred_element_type=F32)
    query_width = query_ref.shape[1] // blocks
    latent_width = down_ref.shape[1] // blocks
    rest = 128 - latent_width
    for k in range(blocks):
        part = slice(k * query_width, (k + 1) * query_width)
        if k * query_width % wide == 0:
            copies[k * query_width // wide].wait()
        query = jnp.dot(rows, query_ref[:, part], preferred_element_type=F32)
        tail = jnp.concatenate(
            [
                latents[:, k * latent_width : (k + 1) * latent_width],
                jnp.broadcast_to(squares, (rows.shape[0], rest)),
            ],
            axis=1,
        )
        for same, ref in ((True, keep_ref), (False, send_ref)):

            @pl.when((core == k % 2) == same)
            def _(ref=ref, query=query, tail=tail):
                ref[k // 2, :, :query_width] = query
                ref[k // 2, :, query_width:] = tail


def new_sums(blocks, one, other, query_proj, down_proj):
    width = query_proj.shape[1] // blocks + 128
    half = jax.ShapeDtypeStruct((blocks // 2, one.shape[0], width), F32)
    return pl.pallas_call(
        functools.partial(new_sums_kernel, blocks),
        out_shape=(half, half),
        in_specs=[pl.BlockSpec(memory_space=pltpu.VMEM)] * 2
        + [pl.BlockSpec(memory_space=pl.ANY), pl.BlockSpec(memory_space=pltpu.VMEM)],
        scratch_shapes=[
            pltpu.VMEM(query_proj.shape, query_proj.dtype),
            pltpu.SemaphoreType.DMA((8,)),
        ],
        compiler_params=pltpu.CompilerParams(vmem_limit_bytes=20 * 1024 * 1024),
        name="new_sums",
    )(one, other, pltpu.with_memory_space_constraint(query_proj, pltpu.HBM), down_proj)


def arrange_kernel(query_width, *refs):
    refs, (query_ref, fresh_ref) = refs[:-2], refs[-2:]
    grid = Grid()
    ys, rows, width = refs[0].shape
    heads = len(refs)
    requests = query_ref.shape[0]
    steps = rows // requests
    cut = width // 2
    each = query_width // HD
    latent_width = cut - query_width
    fresh_ref[...] = jnp.zeros_like(fresh_ref)
    for dz, ref in enumerate(refs):
        for dy in range(ys):
            y = lax.rem(grid.y + ys - dy, ys)
            pair = y * heads + lax.rem(grid.z + heads - dz, heads)
            parts = 2 * each
            first = pair * parts
            g = lax.div(first, HQ // KVH)
            place = lax.rem(first, HQ // KVH) * steps
            for r in range(requests):
                own = []
                for h in range(parts):
                    at = h // each * cut + h % each * HD
                    own.append(ref[dy, r * steps : (r + 1) * steps, at : at + HD])
                start = pl.multiple_of(place, parts * steps)
                query_ref[r, g, pl.ds(start, parts * steps), :] = jnp.concatenate(own, axis=0)
            latents = [
                ref[dy, :, core * cut + query_width : (core + 1) * cut] for core in range(2)
            ]
            latents = jnp.concatenate(latents, axis=1)
            for r in range(requests):
                fresh_ref[r, pair, :steps, :] = latents[r * steps : (r + 1) * steps, :]


def arrange(by_head, requests, query_width):
    ys, rows, width = by_head[0].shape
    steps = rows // requests
    latents = width - 2 * query_width
    return pl.pallas_call(
        functools.partial(arrange_kernel, query_width),
        out_shape=(
            jax.ShapeDtypeStruct((requests, KVH, HQ // KVH * steps, HD), BF),
            jax.ShapeDtypeStruct((requests, ys * len(by_head), FRESH, latents), BF),
        ),
        compiler_params=pltpu.CompilerParams(vmem_limit_bytes=8 * 1024 * 1024),
        name="arrange",
    )(*by_head)


def in_a_box(holds, step, *values):
    shapes = jax.eval_shape(step, *values)

    def otherwise(*_):
        return jax.tree.map(lambda one: jnp.zeros(one.shape, one.dtype), shapes)

    return lax.cond(holds, step, otherwise, *values)


def in_order(parts, mine):
    count = len(parts)
    if count == 2:
        swap = mine == 0
        return jnp.stack([jnp.where(swap, parts[0], parts[1]), jnp.where(swap, parts[1], parts[0])])
    twice = jnp.stack(parts[::-1] * 2)
    return lax.dynamic_slice_in_dim(twice, count - 1 - mine, count, 0)


def local(
    cached_hidden,
    page_order,
    lengths,
    new_ids,
    embedding,
    query_proj,
    down_proj,
    key_up,
    value_up,
    out_proj,
):
    grid = Grid()
    side, y, c, z = grid.side, grid.y, grid.c, grid.z
    ys, heads = grid.ys, grid.heads
    requests, span, width = cached_hidden.shape
    tokens, steps = new_ids.shape
    rows = requests * steps
    depth = down_proj.shape[0]
    hidden = cached_hidden.reshape(requests * span, width)
    hidden = pltpu.with_memory_space_constraint(hidden, pltpu.HBM)
    holds = new_ids[0, 0] >= 0

    def on_cores(*segments):
        return [
            [(rows, dy, dc, dz, base, step) for rows, dy, dz, base, step in segments]
            for dc in range(2)
        ]

    def both(piece, *segments):
        here, there = on_cores(*segments)
        return [(piece, here), (grid.send(piece, core=1), there)]

    def swapped(pieces, at_once=2):
        pairs = []
        for i, piece in enumerate(pieces):
            if i >= at_once:
                piece, _ = tie(piece, pairs[i - at_once][1])
            pairs.append((piece, grid.send(piece, core=1)))
        return pairs

    def add_pairs(pairs, places, latent):
        batch = []
        for pair, segments in zip(pairs, places):
            batch += list(zip(pair, on_cores(*segments)))
        return add_latents(hidden, depth, batch, latent)

    def project_shared(own, between):
        b = depth // 4

        def edge(piece):
            return piece, b, 0, 2 * b

        embed, over_y, over_head, turn, spread_y, spread, lay_out = between
        r0 = first_piece(own, key_up, b)
        r1 = grid.send(r0, head=1)
        y0 = grid.send(r0, y=1)

        extra = in_a_box(holds, lambda ids: over_y(embed(ids)), tie(new_ids, r0)[0])
        r1, y0, extra = tie(r1, y0, extra)

        other = (3 * b, -3 * b)
        at_own = [(4 * b, 0, 0, 0, 0)]
        at_r = [None] + [[(3 * b, 0, k, 0, b)] for k in range(1, heads)]
        at_y = [[(3 * b, 1, k, 0, b)] for k in range(3)] + [[(2 * b, 1, 3, 0, 2 * b)]]
        at_x = [
            None,
            [(b, 0, 1, *other), (b, 1, 0, *other)],
            [(b, 0, 2, *other), (b, 1, 1, *other)],
            [(b, 0, 3, *other), (b, 1, 2, *other)],
            [(2 * b, 1, 3, 2 * b, -2 * b)],
        ]

        r2 = grid.send(r1, head=1)
        y1 = grid.send(r1, y=1)
        (edges,) = assemble([edge(r1), edge(y0)])
        x1 = grid.send(edges, side=1)

        def first_latents(*pieces):
            latent = add_pairs(swapped(pieces), [at_own, at_r[1], at_y[0]], None)
            return latent, r0[3 * b :], r1[3 * b :]

        latent, up0, up1 = in_a_box(holds, first_latents, tie(own, edges)[0], r1, y0)
        r2, y1, x1, latent, extra = tie(r2, y1, x1, latent, extra)

        r3 = grid.send(r2, head=1)
        y2 = grid.send(r2, y=1)
        (edges,) = assemble([edge(r2), edge(y1)])
        x2 = grid.send(edges, side=1)

        def second_latents(pieces, latent, lengths):
            latent = add_pairs(swapped(pieces), [at_r[2], at_y[1], at_x[1]], latent)
            return latent, make_turns(lengths), pieces[0][3 * b :]

        latent, turns, up2 = in_a_box(
            holds, second_latents, (r2, y1, x1), latent, tie(lengths, r2)[0]
        )
        r3, y2, x2, latent = tie(r3, y2, x2, latent)

        last, edges = assemble([(r3, 2 * b, 0, b)], [edge(r3), edge(y2)])
        y3 = grid.send(last, y=1)
        x3 = grid.send(edges, side=1)
        extra, last = tie(extra, last)

        def third_latents(pieces, latent, extra, *turns):
            extra = over_head(extra)
            latent = add_pairs(swapped(pieces), [at_r[3], at_y[2]], latent)
            extra, latent = tie(extra, latent)
            return latent, turn(extra, *turns), pieces[0][3 * b :]

        latent, extra, up3 = in_a_box(holds, third_latents, (r3, y2), latent, extra, *turns)
        x2, x3, y3, latent, extra = tie(x2, x3, y3, latent, extra)

        x4 = grid.send(y3, side=1)

        def fourth_latents(pieces, latent, extra):
            extra = spread_y(extra)
            pairs = swapped(pieces)
            extra, pairs = tie(extra, pairs)
            latent = add_pairs(pairs, [at_x[2], at_y[3], at_x[3]], latent)
            return latent, lay_out(spread(extra))

        latent, extra = in_a_box(holds, fourth_latents, (x2, y3, x3), latent, extra)
        x4, latent, extra = tie(x4, latent, extra)
        batch = list(zip((x4, grid.send(x4, core=1)), on_cores(*at_x[4])))
        return batch, latent, (extra, ([up0, up1, up2, up3], 0), turns)

    def project_plain(own, between):
        latent = None
        ring = own
        for k in range(heads):
            if k:
                ring = grid.send(ring, head=1)
            if k:
                latent = add_latents(hidden, depth, batch, latent)
            batch = both(ring, (depth, 0, k, 0, 0))
            for dy in range(1, ys):
                latent = add_latents(hidden, depth, batch, latent)
                batch = both(grid.send(ring, y=dy), (depth, dy, k, 0, 0))
        turns = make_turns(lengths)
        embed, over_y, over_head, turn, spread_y, spread, lay_out = between
        extra = turn(over_head(over_y(embed(new_ids))), *turns)
        extra = lay_out(spread(spread_y(extra)))
        ups = [pack_up(key_up)]
        ups += [grid.send(ups[0], head=k) for k in range(1, heads)]
        return batch, latent, (extra, (ups, 0), turns)

    blocks = 2 * ys * heads
    query_width = query_proj.shape[1] // blocks
    latent_width = down_proj.shape[1] // blocks
    cut = query_width + latent_width

    def embed(ids):
        keep, rest = pick(ids, embedding)
        keep, rest = new_sums(blocks, keep, grid.send(rest, side=1), query_proj, down_proj)
        packed = keep + grid.send(rest, core=1)
        return packed.reshape(ys, heads, rows, -1)

    def reduce_over_y(packed):
        kept = take(packed, y)
        for dy in range(1, ys):
            kept = kept + grid.send(take(packed, (y + dy) % ys), y=dy)
        return kept

    def reduce_over_head(kept):
        return lax.all_to_all(kept, "head", 0, 0)

    def turn(sums, cosine, sines):
        block = turn_query(sums, cosine, sines, query_width, latent_width)
        pair = in_order([block, grid.send(block, core=1)], c)
        return jnp.concatenate([pair[0], pair[1]], axis=-1)

    def spread_over_y(pair):
        return jnp.stack([pair] + [grid.send(pair, y=k) for k in range(1, ys)])

    def spread_over_head(by_y):
        return [by_y] + [grid.send(by_y, head=k) for k in range(1, heads)]

    def lay_out(by_head):
        return arrange(by_head, requests, query_width)

    pages = page_order.shape[1]
    start = ((y * 2 + c) * heads + z) * span

    def make_turns(lengths):
        fresh_positions = lengths[:, None] + jnp.arange(steps, dtype=jnp.int32)[None, :]
        positions = [
            start + PAGE * jnp.arange(pages, dtype=jnp.int32),
            jnp.arange(16 - pages % 16 if pages % 16 else 0, dtype=jnp.int32),
            jnp.arange(PAGE, dtype=jnp.int32),
            fresh_positions.reshape(-1),
        ]
        return sincos(jnp.concatenate(positions))

    between = [
        embed, reduce_over_y, reduce_over_head, turn, spread_over_y, spread_over_head, lay_out,
    ]
    shared = ys == 2 and heads == 4 and grid.sides == 2 and depth % 512 == 0
    batch, latent, extra = (project_shared if shared else project_plain)(down_proj, between)
    (queries, fresh), (ups, up_row), (cosine, sines) = extra
    weight = pltpu.with_memory_space_constraint(out_proj, pltpu.HBM)
    states, weight = finish(
        span, hidden, depth, batch, latent, fresh, cosine, sines, queries, ups, up_row, weight,
        heads, page_order, lengths, steps,
    )
    parts = [take(states, z)]
    for dz in range(1, heads):
        parts.append(grid.send(take(states, (z + dz) % heads), head=dz))
    state = join_parts(parts)
    states = [state]
    for dy in range(ys):
        for dc in range(2):
            if dy or dc:
                states.append(grid.send(state, y=dy, core=dc))
    partial_out = project_out(states, value_up, weight, requests, steps)
    sent = partial_out.astype(BF)
    attended = partial_out
    for dz in range(1, heads):
        attended = attended + grid.send(sent, head=dz).astype(F32)
    return attended.astype(BF).reshape(requests, steps, -1)


def solution(mesh):
    return jax.shard_map(
        local,
        mesh=mesh,
        in_specs=(
            P("side", ("seq", "head"), None),
            P("side", ("seq", "head")),
            P("side"),
            P(),
            P("side", ("seq", "head")),
            P(("seq", "head"), None),
            P(("seq", "head"), None),
            P("head", None, None),
            P("head", None, None),
            P("head", "seq"),
        ),
        out_specs=P("side", None, "seq"),
        check_vma=False,
    )
```

```python
import functools
import math

import jax
import jax.numpy as jnp
from jax import lax
from jax.experimental import pallas as pl
from jax.experimental.pallas import tpu as pltpu
from jax.sharding import PartitionSpec as P

D = 8192
HQ = 64
KVH = 8
HD = 128
RANK = 64
PAGE = 16
FRESH = 16

AXES = ("side", "seq", "head")
rope_base = 500000.0
masked_score = -1e30
BF = jnp.bfloat16
F32 = jnp.float32


def sincos(positions):
    half = HD // 2
    frequency = 1.0 / rope_base ** (jnp.arange(half, dtype=F32) * 2.0 / HD)
    angles = positions.astype(F32)[..., None] * frequency
    cosine, sines = jnp.cos(angles), jnp.sin(angles)
    return (
        jnp.concatenate([cosine, cosine], axis=-1),
        jnp.concatenate([-sines, sines], axis=-1),
    )


class Grid:
    def __init__(self):
        self.sides, self.seqs, self.heads = (lax.axis_size(a) for a in AXES)
        self.ys = self.seqs // 2
        self.side, seq, self.z = (lax.axis_index(a) for a in AXES)
        self.y, self.c = lax.div(seq, 2), lax.rem(seq, 2)

    def send(self, value, side=0, y=0, core=0, head=0):
        pairs = []
        for a in range(self.sides):
            for b in range(self.ys):
                for c in range(2):
                    for d in range(self.heads):
                        to = (
                            (a + side) % self.sides,
                            (b + y) % self.ys,
                            (c + core) % 2,
                            (d + head) % self.heads,
                        )
                        pairs.append((self.flat(a, b, c, d), self.flat(*to)))
        return lax.ppermute(value, AXES, pairs)

    def along_heads(self, value_for):
        sent = {}
        for k in sorted(range(1, self.heads), key=lambda k: -min(k, self.heads - k)):
            sent[k] = self.send(value_for(k), head=k)
        return [sent[k] for k in range(1, self.heads)]

    def place(self, dy, dc, dz):
        seq = lax.rem(self.y + self.ys - dy, self.ys) * 2 + (1 - self.c if dc else self.c)
        return seq * self.heads + lax.rem(self.z + self.heads - dz, self.heads)

    def flat(self, a, b, c, d):
        return (a * self.seqs + b * 2 + c) * self.heads + d


def accumulate(
    counts, segments, depth, hidden_ref, pieces, before_ref, hidden_buf, piece_buf, total, sems, store=None
):
    grid = Grid()
    rows = hidden_ref.shape[0]
    if before_ref is not None:
        load = pltpu.make_async_copy(before_ref, total, sems.at[len(segments) + len(pieces)])
    waits = []
    at = 0
    for i, count in enumerate(counts):
        copies = [
            pltpu.make_async_copy(
                pieces[i].at[pl.ds(0, count), :],
                piece_buf.at[pl.ds(at, count), :],
                sems.at[len(segments) + i],
            )
        ]
        inside = 0
        for k, (owner, extent, dy, dc, dz, base, step) in enumerate(segments):
            if owner == i:
                source = grid.place(dy, dc, dz) * depth + base + step * grid.side
                source = pl.multiple_of(source, 128)
                copies.append(
                    pltpu.make_async_copy(
                        hidden_ref.at[:, pl.ds(source, extent)],
                        hidden_buf.at[:, pl.ds(at + inside, extent)],
                        sems.at[k],
                    )
                )
                inside += extent
        for copy in copies:
            copy.start()
        if before_ref is not None and i == 1:
            load.start()
        waits.append((copies, at, count))
        at += count
    pairs = [waits[i : i + 2] for i in range(0, len(waits), 2)]
    for k, pair in enumerate(pairs):
        for copies, _, _ in pair:
            for copy in copies:
                copy.wait()
        first = pair[0][1]
        span = sum(count for _, _, count in pair)
        last = k == len(pairs) - 1
        tile = rows // 4 if last and store else rows
        for m in range(rows // tile):
            part = slice(m * tile, (m + 1) * tile)
            term = jnp.dot(
                hidden_buf[part, first : first + span],
                piece_buf[first : first + span, :],
                preferred_element_type=F32,
            )
            if k == 0 and m == 0 and before_ref is not None:
                load.wait()
            total[part, :] = total[part, :] + term if k or before_ref is not None else term
            if last and store:
                store(m, tile)


def latent_kernel(counts, segments, depth, has_total, hidden_ref, *refs):
    pieces, refs = refs[: len(counts)], refs[len(counts) :]
    before_ref = None
    if has_total:
        before_ref, refs = refs[0], refs[1:]
    out_ref, hidden_buf, piece_buf, total, sems, out_sems = refs
    stores = []

    def store(m, tile):
        rows = pl.ds(m * tile, tile)
        copy = pltpu.make_async_copy(total.at[rows, :], out_ref.at[rows, :], out_sems.at[m])
        copy.start()
        stores.append(copy)

    accumulate(
        counts, segments, depth, hidden_ref, pieces, before_ref, hidden_buf, piece_buf, total, sems, store
    )
    for copy in stores:
        copy.wait()


def add_latents(hidden, depth, batch, total=None):
    pieces = [piece for piece, _ in batch]
    counts = [sum(part[0] for part in parts) for _, parts in batch]
    segments = [(i, *part) for i, (_, parts) in enumerate(batch) for part in parts]
    deep, columns = sum(counts), pieces[0].shape[1]
    rows = hidden.shape[0]
    operands = [hidden, *pieces]
    if total is not None:
        operands.append(total)
    return pl.pallas_call(
        functools.partial(latent_kernel, counts, segments, depth, total is not None),
        out_shape=jax.ShapeDtypeStruct((rows, columns), F32),
        in_specs=[pl.BlockSpec(memory_space=pl.ANY)] * len(operands),
        out_specs=pl.BlockSpec(memory_space=pl.ANY),
        scratch_shapes=[
            pltpu.VMEM((rows, deep), BF),
            pltpu.VMEM((deep, columns), BF),
            pltpu.VMEM((rows, columns), F32),
            pltpu.SemaphoreType.DMA((len(segments) + len(pieces) + 1,)),
            pltpu.SemaphoreType.DMA((4,)),
        ],
        compiler_params=pltpu.CompilerParams(vmem_limit_bytes=28 * 1024 * 1024),
        cost_estimate=pl.CostEstimate(
            flops=2 * rows * deep * columns,
            bytes_accessed=2 * deep * (rows + columns) + 8 * rows * columns,
            transcendentals=0,
        ),
        name="latents",
    )(*operands)


def first_piece_kernel(rows, own_ref, up_ref, out_ref, sems):
    side = lax.axis_index("side")
    groups = up_ref.shape[0]
    each = RANK // FRESH
    start = pl.multiple_of(rows * side, 16)
    copies = [
        pltpu.make_async_copy(
            own_ref.at[pl.ds(start, 3 * rows), :], out_ref.at[pl.ds(0, 3 * rows), :], sems.at[0]
        )
    ]
    for k in range(groups * each):
        copies.append(
            pltpu.make_async_copy(
                up_ref.at[k // each, pl.ds(k % each * FRESH, FRESH), :],
                out_ref.at[pl.ds(3 * rows, FRESH), pl.ds(k * HD, HD)],
                sems.at[1 + k],
            )
        )
    for copy in copies:
        copy.start()
    for copy in copies:
        copy.wait()


def first_piece(own, key_up, rows):
    count = key_up.shape[0] * RANK // FRESH
    return pl.pallas_call(
        functools.partial(first_piece_kernel, rows),
        out_shape=jax.ShapeDtypeStruct((3 * rows + FRESH, own.shape[1]), own.dtype),
        in_specs=[pl.BlockSpec(memory_space=pl.ANY)] * 2,
        out_specs=pl.BlockSpec(memory_space=pltpu.VMEM),
        scratch_shapes=[pltpu.SemaphoreType.DMA((1 + count,))],
        compiler_params=pltpu.CompilerParams(vmem_limit_bytes=8 * 1024 * 1024),
        cost_estimate=pl.CostEstimate(flops=1, bytes_accessed=1, transcendentals=0),
        name="first_piece",
    )(own, key_up)


def assemble_kernel(layout, *refs):
    ins, outs, sems = refs[: len(layout)], refs[len(layout) : -1], refs[-1]
    side = lax.axis_index("side")
    copies = []
    for k, (o, at, count, base, step) in enumerate(layout):
        start = pl.multiple_of(base + step * side, 16)
        copies.append(
            pltpu.make_async_copy(
                ins[k].at[pl.ds(start, count), :], outs[o].at[pl.ds(at, count), :], sems.at[k]
            )
        )
        copies[-1].start()
    for copy in copies:
        copy.wait()


def assemble(*arrays):
    layout, sources, shapes = [], [], []
    for o, parts in enumerate(arrays):
        at = 0
        for source, count, base, step in parts:
            layout.append((o, at, count, base, step))
            sources.append(source)
            at += count
        shapes.append(jax.ShapeDtypeStruct((at, source.shape[1]), source.dtype))
    return pl.pallas_call(
        functools.partial(assemble_kernel, layout),
        out_shape=shapes,
        in_specs=[pl.BlockSpec(memory_space=pl.ANY)] * len(sources),
        out_specs=[pl.BlockSpec(memory_space=pltpu.VMEM)] * len(shapes),
        scratch_shapes=[pltpu.SemaphoreType.DMA((len(layout),))],
        compiler_params=pltpu.CompilerParams(vmem_limit_bytes=8 * 1024 * 1024),
        cost_estimate=pl.CostEstimate(flops=1, bytes_accessed=1, transcendentals=0),
        name="assemble",
    )(*sources)


def in_three(value):
    high = value.astype(BF).astype(F32)
    middle = (value - high).astype(BF).astype(F32)
    return high, middle, value - high - middle


def pack_up(key_up):
    groups = key_up.shape[0]
    parts = key_up.reshape(groups, RANK // FRESH, FRESH, HD).transpose(2, 0, 1, 3)
    return parts.reshape(FRESH, -1)


def unpack_up(up_ref, g):
    each = up_ref.shape[2] // (RANK // FRESH * HD)
    at = g % each * (RANK // FRESH)
    parts = [up_ref[g // each, :, (at + i) * HD : (at + i + 1) * HD] for i in range(RANK // FRESH)]
    return jnp.concatenate(parts, axis=0)


def attend_part(scale, span, lat_ref, fresh_ref, cos_ref, sin_ref, live_ref, query_ref, up_ref, out_ref):
    requests, groups, lanes, _ = query_ref.shape
    blocks = out_ref.shape[0]
    each = groups // blocks
    peaks, totals, summed = [], [], []
    ups = [unpack_up(up_ref, g) for g in range(groups)]
    for r in range(requests):
        latent = jnp.concatenate(
            [
                lat_ref[r * span : (r + 1) * span, :].astype(BF),
                jnp.concatenate([fresh_ref[r, p] for p in range(fresh_ref.shape[1])], axis=1),
            ],
            axis=0,
        )
        cosine, sines = cos_ref[r], sin_ref[r]
        columns, values = [], []
        for g in range(groups):
            at = g * 2 * RANK
            key = jnp.dot(latent[:, at : at + RANK], ups[g], preferred_element_type=F32)
            key = (key * cosine + pltpu.roll(key, HD // 2, 1) * sines).astype(BF)
            columns.append(
                lax.dot_general(
                    key, query_ref[r, g], (((1,), (1,)), ((), ())), preferred_element_type=F32
                )
            )
            values.append(latent[:, at + RANK : at + 2 * RANK])
        scores = jnp.concatenate(columns, axis=1) * scale
        live = live_ref[r] > 0
        live = jnp.concatenate([live] * (scores.shape[1] // live.shape[1]), axis=1)
        scores = jnp.where(live, scores, masked_score)
        peak = jnp.max(scores, axis=0, keepdims=True)
        weights = jnp.where(live, jnp.exp(scores - peak), 0.0)
        peaks.append(peak)
        totals.append(jnp.sum(weights, axis=0, keepdims=True))
        summed.append(
            lax.dot_general(
                jnp.concatenate(values, axis=1),
                weights.astype(BF),
                (((0,), (0,)), ((), ())),
                preferred_element_type=F32,
            )
        )
    for b in range(blocks):
        stats = []
        for i in range(each):
            g = b * each + i
            cut = slice(g * lanes, (g + 1) * lanes)
            out_ref[b, i * RANK : (i + 1) * RANK, :] = jnp.concatenate(
                [s[g * RANK : (g + 1) * RANK, cut] for s in summed], axis=1
            ).astype(BF)
            stats += in_three(jnp.concatenate([p[:, cut] for p in peaks], axis=1))
            stats += in_three(jnp.concatenate([t[:, cut] for t in totals], axis=1))
        stats += [jnp.zeros_like(stats[0])] * (16 - len(stats))
        out_ref[b, each * RANK :, :] = jnp.concatenate(stats, axis=0).astype(BF)


def lay_tables(span, steps, start, order_ref, length_ref, small_cos, small_sin, cos_ref, sin_ref, live_ref):
    requests, rows, lanes = cos_ref.shape
    pages = order_ref.shape[1]
    padded = -(-pages // 16) * 16
    inner_cos, inner_sin = small_cos[padded : padded + PAGE, :], small_sin[padded : padded + PAGE, :]
    inner = lax.broadcasted_iota(jnp.int32, (PAGE, lanes), 0)
    grid = Grid()
    first = grid.place(0, 0, 0) == 0
    column_step = lax.rem(lax.broadcasted_iota(jnp.int32, (FRESH, lanes), 1), steps)
    new_row = lax.broadcasted_iota(jnp.int32, (FRESH, lanes), 0)
    seen = jnp.where(jnp.logical_and(new_row <= column_step, first), 1.0, 0.0)
    for j in range(pages):
        page_cos, page_sin = small_cos[j : j + 1, :], small_sin[j : j + 1, :]
        cosine = page_cos * inner_cos - page_sin * inner_sin
        sines = page_sin * inner_cos + page_cos * inner_sin
        for r in range(requests):
            at = pl.multiple_of(order_ref[r, j] * PAGE, PAGE)
            cos_ref[r, pl.ds(at, PAGE), :] = cosine
            sin_ref[r, pl.ds(at, PAGE), :] = sines
            position = start + j * PAGE + inner
            live_ref[r, pl.ds(at, PAGE), :] = jnp.where(position < length_ref[r], 1.0, 0.0)
    fill = jnp.zeros((FRESH - steps, lanes), F32)
    new = padded + PAGE
    for r in range(requests):
        own = slice(new + r * steps, new + (r + 1) * steps)
        cos_ref[r, span:, :] = jnp.concatenate([small_cos[own, :], fill], axis=0)
        sin_ref[r, span:, :] = jnp.concatenate([small_sin[own, :], fill], axis=0)
        live_ref[r, span:, :] = seen


def finish_kernel(counts, segments, depth, scale, span, up_row, steps, order_ref, length_ref, *refs):
    small_cos, small_sin, hidden_ref, refs = refs[0], refs[1], refs[2], refs[3:]
    pieces, refs = refs[: len(counts)], refs[len(counts) :]
    heads = lax.axis_size("head")
    before_ref, tables, ups, weight_ref = refs[0], refs[1:3], refs[3 : 3 + heads], refs[3 + heads]
    out_ref, weight_out, hidden_buf, piece_buf, total, *refs = refs[4 + heads :]
    held, (cos_ref, sin_ref, live_ref, up_buf, sems, table_sems, weight_sem) = refs[:2], refs[2:]
    loads = [
        pltpu.make_async_copy(table, buf, table_sems.at[i])
        for i, (table, buf) in enumerate(zip(tables, held))
    ]
    z = lax.axis_index("head")
    for k, up in enumerate(ups):
        place = lax.rem(z + heads - k, heads)
        loads.append(
            pltpu.make_async_copy(
                up.at[pl.ds(up_row, FRESH), :], up_buf.at[place], table_sems.at[len(tables) + k]
            )
        )
    for load in loads:
        load.start()
    grid = Grid()
    start = grid.place(0, 0, 0) * span
    lay_tables(
        span, steps, start, order_ref, length_ref, small_cos, small_sin, cos_ref, sin_ref, live_ref
    )
    accumulate(counts, segments, depth, hidden_ref, pieces, before_ref, hidden_buf, piece_buf, total, sems)
    for load in loads:
        load.wait()
    bring = pltpu.make_async_copy(weight_ref, weight_out, weight_sem)
    bring.start()
    fresh, queries = held
    attend_part(scale, span, total, fresh, cos_ref, sin_ref, live_ref, queries, up_buf, out_ref)
    bring.wait()


def finish(
    span, hidden, depth, batch, total, fresh, cosine, sines, queries, ups, up_row, weight, blocks,
    page_order, lengths, steps,
):
    pieces = [piece for piece, _ in batch]
    counts = [sum(part[0] for part in parts) for _, parts in batch]
    segments = [(i, *part) for i, (_, parts) in enumerate(batch) for part in parts]
    deep, columns = sum(counts), pieces[0].shape[1]
    rows = hidden.shape[0]
    requests, groups, lanes, _ = queries.shape
    tables = (fresh, queries)
    wide = (requests, span + FRESH, HD)
    total = pltpu.with_memory_space_constraint(total, pltpu.VMEM)
    operands = [page_order, lengths, cosine, sines, hidden, *pieces, total, *tables, *ups, weight]
    far = [pl.BlockSpec(memory_space=pl.ANY)] * (len(operands) - 4)
    state_rows = groups // blocks * RANK + 16
    return pl.pallas_call(
        functools.partial(
            finish_kernel, counts, segments, depth, 1.0 / math.sqrt(HD), span, up_row, steps
        ),
        out_shape=(
            jax.ShapeDtypeStruct((blocks, state_rows, requests * lanes), BF),
            pltpu.VMEM(weight.shape, weight.dtype),
        ),
        in_specs=[pl.BlockSpec(memory_space=pltpu.SMEM)] * 2
        + [pl.BlockSpec(memory_space=pltpu.VMEM)] * 2
        + far,
        out_specs=(pl.BlockSpec(memory_space=pltpu.VMEM), pl.BlockSpec(memory_space=pl.ANY)),
        scratch_shapes=[
            pltpu.VMEM((rows, deep), BF),
            pltpu.VMEM((deep, columns), BF),
            pltpu.VMEM((rows, columns), F32),
        ]
        + [pltpu.VMEM(table.shape, table.dtype) for table in tables]
        + [pltpu.VMEM(wide, F32)] * 3
        + [
            pltpu.VMEM((len(ups), FRESH, ups[0].shape[1]), BF),
            pltpu.SemaphoreType.DMA((len(segments) + len(pieces) + 1,)),
            pltpu.SemaphoreType.DMA((len(tables) + len(ups),)),
            pltpu.SemaphoreType.DMA,
        ],
        compiler_params=pltpu.CompilerParams(vmem_limit_bytes=18 * 1024 * 1024),
        cost_estimate=pl.CostEstimate(flops=1, bytes_accessed=1, transcendentals=0),
        name="finish",
    )(*operands)


def join(states):
    peak = functools.reduce(jnp.maximum, [p for p, _, _ in states])
    total, summed = 0.0, 0.0
    for p, t, s in states:
        weight = jnp.exp(p - peak)
        total = total + t * weight
        summed = summed + s * weight
    return peak, total, summed


def pack(states, out_ref):
    each = len(states)
    stats = []
    for i, (peak, total, summed) in enumerate(states):
        out_ref[i * RANK : (i + 1) * RANK, :] = summed.astype(BF)
        stats += [*in_three(peak), *in_three(total)]
    stats += [jnp.zeros_like(stats[0])] * (16 - len(stats))
    out_ref[each * RANK :, :] = jnp.concatenate(stats, axis=0).astype(BF)


def unpack(ref, each):
    stats = ref[each * RANK :, :].astype(F32)
    states = []
    for i in range(each):
        three = [stats[at : at + 1] for at in range(6 * i, 6 * i + 6)]
        peak, total = three[0] + three[1] + three[2], three[3] + three[4] + three[5]
        states.append((peak, total, ref[i * RANK : (i + 1) * RANK, :].astype(F32)))
    return states


def join_parts_kernel(each, *refs):
    refs, out_ref = refs[:-1], refs[-1]
    parts = [unpack(ref, each) for ref in refs]
    pack([join([part[i] for part in parts]) for i in range(each)], out_ref)


def join_parts(parts):
    return pl.pallas_call(
        functools.partial(join_parts_kernel, (parts[0].shape[0] - 16) // RANK),
        out_shape=jax.ShapeDtypeStruct(parts[0].shape, BF),
        compiler_params=pltpu.CompilerParams(vmem_limit_bytes=4 * 1024 * 1024),
        cost_estimate=pl.CostEstimate(flops=1, bytes_accessed=1, transcendentals=0),
        name="join_parts",
    )(*parts)


def project_out_kernel(requests, steps, *refs):
    up_ref, weight_ref, out_ref = refs[-3:]
    each = up_ref.shape[0]
    parts = [unpack(ref, each) for ref in refs[:-3]]
    lanes = refs[0].shape[1]
    rows = requests * steps
    heads = lanes // rows
    old = lax.broadcasted_iota(jnp.int32, (lanes, lanes), 0)
    new = lax.broadcasted_iota(jnp.int32, (lanes, lanes), 1)
    request, rest = old // (heads * steps), old % (heads * steps)
    moved = (rest // steps) * rows + request * steps + rest % steps
    order = jnp.where(moved == new, 1.0, 0.0).astype(BF)
    context = []
    for i in range(each):
        _, total, summed = join([part[i] for part in parts])
        scaled = (summed / total).astype(BF)
        one = lax.dot_general(
            up_ref[i], scaled, (((0,), (0,)), ((), ())), preferred_element_type=F32
        ).astype(BF)
        one = lax.dot_general(
            order, one, (((0,), (1,)), ((), ())), preferred_element_type=F32
        ).astype(BF)
        context += [one[j * rows : (j + 1) * rows, :] for j in range(heads)]
    out_ref[...] = jnp.dot(
        jnp.concatenate(context, axis=1), weight_ref[...], preferred_element_type=F32
    )


def project_out(parts, value_up, out_proj, requests, steps):
    return pl.pallas_call(
        functools.partial(project_out_kernel, requests, steps),
        out_shape=jax.ShapeDtypeStruct((requests * steps, out_proj.shape[1]), F32),
        compiler_params=pltpu.CompilerParams(vmem_limit_bytes=24 * 1024 * 1024),
        cost_estimate=pl.CostEstimate(flops=1, bytes_accessed=1, transcendentals=0),
        name="project_out",
    )(*parts, value_up, out_proj)


def take(stack, index, axis=0):
    return lax.dynamic_index_in_dim(stack, index, axis, keepdims=False)


def tie(*values):
    leaves, tree = jax.tree.flatten(values)
    arrays = [i for i, leaf in enumerate(leaves) if getattr(leaf, "ndim", 0)]
    for i, leaf in zip(arrays, lax.optimization_barrier([leaves[i] for i in arrays])):
        leaves[i] = leaf
    return jax.tree.unflatten(tree, leaves)


def turn_query_kernel(query_width, latent_width, sums_ref, cos_ref, sin_ref, out_ref):
    sums = sums_ref[0]
    for k in range(1, sums_ref.shape[0]):
        sums = sums + sums_ref[k]
    at = query_width + latent_width
    sums = sums * lax.rsqrt(sums[:, at : at + 1] / D + 1e-05)
    own = slice(cos_ref.shape[0] - sums.shape[0], None)
    cosine, sines = cos_ref[own, :], sin_ref[own, :]
    for h in range(query_width // HD):
        one = sums[:, h * HD : (h + 1) * HD]
        one = one * cosine + pltpu.roll(one, HD // 2, 1) * sines
        out_ref[:, h * HD : (h + 1) * HD] = one.astype(BF)
    out_ref[:, query_width:at] = sums[:, query_width:at].astype(BF)


def turn_query(sums, cosine, sines, query_width, latent_width):
    return pl.pallas_call(
        functools.partial(turn_query_kernel, query_width, latent_width),
        out_shape=jax.ShapeDtypeStruct((sums.shape[1], query_width + latent_width), BF),
        compiler_params=pltpu.CompilerParams(vmem_limit_bytes=4 * 1024 * 1024),
        name="turn_query",
    )(sums, cosine, sines)


def pick_kernel(ids_ref, table_ref, keep_ref, send_ref, buf, sems):
    side = lax.axis_index("side")
    rows = table_ref.shape[0]
    steps, requests = ids_ref.shape
    count = requests * steps
    places = []
    for i in range(count):
        place = ids_ref[i % steps, i // steps] - side * rows
        inside = jnp.logical_and(place >= 0, place < rows)
        place = jnp.where(inside, place, 0)
        start = pl.multiple_of(lax.div(place, FRESH) * FRESH, FRESH)
        pltpu.make_async_copy(table_ref.at[pl.ds(start, FRESH), :], buf.at[i], sems.at[i]).start()
        places.append(jnp.where(inside, place - start, FRESH))
    row = lax.broadcasted_iota(jnp.int32, buf.shape[1:], 0)
    for half in range(2):
        picked = []
        for i in range(half * count // 2, (half + 1) * count // 2):
            pltpu.make_async_copy(table_ref.at[pl.ds(0, FRESH), :], buf.at[i], sems.at[i]).wait()
            one = jnp.where(row == places[i], buf[i].astype(F32), 0.0)
            picked.append(jnp.sum(one, axis=0, keepdims=True))
        picked = jnp.concatenate(picked, axis=0).astype(BF)

        @pl.when(side == half)
        def _():
            keep_ref[...] = picked

        @pl.when(side != half)
        def _():
            send_ref[...] = picked


def pick(ids, table):
    width = table.shape[1]
    half = jax.ShapeDtypeStruct((ids.size // 2, width), BF)
    return pl.pallas_call(
        pick_kernel,
        out_shape=(half, half),
        in_specs=[pl.BlockSpec(memory_space=pltpu.SMEM), pl.BlockSpec(memory_space=pl.ANY)],
        scratch_shapes=[
            pltpu.VMEM((ids.size, FRESH, width), BF),
            pltpu.SemaphoreType.DMA((ids.size,)),
        ],
        compiler_params=pltpu.CompilerParams(vmem_limit_bytes=4 * 1024 * 1024),
        name="pick",
    )(ids, table)


def new_sums_kernel(
    blocks, one_ref, other_ref, query_far, down_ref, keep_ref, send_ref, query_ref, sems
):
    wide = query_ref.shape[1] // sems.shape[0]
    copies = []
    for k in range(sems.shape[0]):
        part = pl.ds(k * wide, wide)
        copies.append(
            pltpu.make_async_copy(query_far.at[:, part], query_ref.at[:, part], sems.at[k])
        )
        copies[-1].start()
    core = lax.rem(lax.axis_index("seq"), 2)
    rows = one_ref[...] + other_ref[...]
    widened = rows.astype(F32)
    squares = jnp.sum(widened * widened, axis=1, keepdims=True)
    latents = jnp.dot(rows, down_ref[...], preferred_element_type=F32)
    query_width = query_ref.shape[1] // blocks
    latent_width = down_ref.shape[1] // blocks
    rest = 128 - latent_width
    for k in range(blocks):
        part = slice(k * query_width, (k + 1) * query_width)
        if k * query_width % wide == 0:
            copies[k * query_width // wide].wait()
        query = jnp.dot(rows, query_ref[:, part], preferred_element_type=F32)
        tail = jnp.concatenate(
            [
                latents[:, k * latent_width : (k + 1) * latent_width],
                jnp.broadcast_to(squares, (rows.shape[0], rest)),
            ],
            axis=1,
        )
        for same, ref in ((True, keep_ref), (False, send_ref)):

            @pl.when((core == k % 2) == same)
            def _(ref=ref, query=query, tail=tail):
                ref[k // 2, :, :query_width] = query
                ref[k // 2, :, query_width:] = tail


def new_sums(blocks, one, other, query_proj, down_proj):
    width = query_proj.shape[1] // blocks + 128
    half = jax.ShapeDtypeStruct((blocks // 2, one.shape[0], width), F32)
    return pl.pallas_call(
        functools.partial(new_sums_kernel, blocks),
        out_shape=(half, half),
        in_specs=[pl.BlockSpec(memory_space=pltpu.VMEM)] * 2
        + [pl.BlockSpec(memory_space=pl.ANY), pl.BlockSpec(memory_space=pltpu.VMEM)],
        scratch_shapes=[
            pltpu.VMEM(query_proj.shape, query_proj.dtype),
            pltpu.SemaphoreType.DMA((8,)),
        ],
        compiler_params=pltpu.CompilerParams(vmem_limit_bytes=20 * 1024 * 1024),
        name="new_sums",
    )(one, other, pltpu.with_memory_space_constraint(query_proj, pltpu.HBM), down_proj)


def arrange_kernel(query_width, *refs):
    refs, (query_ref, fresh_ref) = refs[:-2], refs[-2:]
    grid = Grid()
    ys, rows, width = refs[0].shape
    heads = len(refs)
    requests = query_ref.shape[0]
    steps = rows // requests
    cut = width // 2
    each = query_width // HD
    latent_width = cut - query_width
    fresh_ref[...] = jnp.zeros_like(fresh_ref)
    for dz, ref in enumerate(refs):
        for dy in range(ys):
            y = lax.rem(grid.y + ys - dy, ys)
            pair = y * heads + lax.rem(grid.z + heads - dz, heads)
            parts = 2 * each
            first = pair * parts
            g = lax.div(first, HQ // KVH)
            place = lax.rem(first, HQ // KVH) * steps
            for r in range(requests):
                own = []
                for h in range(parts):
                    at = h // each * cut + h % each * HD
                    own.append(ref[dy, r * steps : (r + 1) * steps, at : at + HD])
                start = pl.multiple_of(place, parts * steps)
                query_ref[r, g, pl.ds(start, parts * steps), :] = jnp.concatenate(own, axis=0)
            latents = [
                ref[dy, :, core * cut + query_width : (core + 1) * cut] for core in range(2)
            ]
            latents = jnp.concatenate(latents, axis=1)
            for r in range(requests):
                fresh_ref[r, pair, :steps, :] = latents[r * steps : (r + 1) * steps, :]


def arrange(by_head, requests, query_width):
    ys, rows, width = by_head[0].shape
    steps = rows // requests
    latents = width - 2 * query_width
    return pl.pallas_call(
        functools.partial(arrange_kernel, query_width),
        out_shape=(
            jax.ShapeDtypeStruct((requests, KVH, HQ // KVH * steps, HD), BF),
            jax.ShapeDtypeStruct((requests, ys * len(by_head), FRESH, latents), BF),
        ),
        compiler_params=pltpu.CompilerParams(vmem_limit_bytes=8 * 1024 * 1024),
        name="arrange",
    )(*by_head)


def in_a_box(holds, step, *values):
    shapes = jax.eval_shape(step, *values)

    def otherwise(*_):
        return jax.tree.map(lambda one: jnp.zeros(one.shape, one.dtype), shapes)

    return lax.cond(holds, step, otherwise, *values)


def in_order(parts, mine):
    count = len(parts)
    if count == 2:
        swap = mine == 0
        return jnp.stack([jnp.where(swap, parts[0], parts[1]), jnp.where(swap, parts[1], parts[0])])
    twice = jnp.stack(parts[::-1] * 2)
    return lax.dynamic_slice_in_dim(twice, count - 1 - mine, count, 0)


def local(
    cached_hidden,
    page_order,
    lengths,
    new_ids,
    embedding,
    query_proj,
    down_proj,
    key_up,
    value_up,
    out_proj,
):
    grid = Grid()
    side, y, c, z = grid.side, grid.y, grid.c, grid.z
    ys, heads = grid.ys, grid.heads
    requests, span, width = cached_hidden.shape
    tokens, steps = new_ids.shape
    rows = requests * steps
    depth = down_proj.shape[0]
    hidden = cached_hidden.reshape(requests * span, width)
    hidden = pltpu.with_memory_space_constraint(hidden, pltpu.HBM)
    ids_by_step = new_ids.T
    holds = ids_by_step[0, 0] >= 0

    def on_cores(*segments):
        return [
            [(rows, dy, dc, dz, base, step) for rows, dy, dz, base, step in segments]
            for dc in range(2)
        ]

    def both(piece, *segments):
        here, there = on_cores(*segments)
        return [(piece, here), (grid.send(piece, core=1), there)]

    def swapped(pieces, at_once=2):
        pairs = []
        for i, piece in enumerate(pieces):
            if i >= at_once:
                piece, _ = tie(piece, pairs[i - at_once][1])
            pairs.append((piece, grid.send(piece, core=1)))
        return pairs

    def add_pairs(pairs, places, latent):
        batch = []
        for pair, segments in zip(pairs, places):
            batch += list(zip(pair, on_cores(*segments)))
        return add_latents(hidden, depth, batch, latent)

    def project_shared(own, between):
        b = depth // 4

        def edge(piece):
            return piece, b, 0, 2 * b

        embed, over_y, over_head, turn, spread_y, spread, lay_out = between
        r0 = first_piece(own, key_up, b)
        r1 = grid.send(r0, head=1)
        y0 = grid.send(r0, y=1)

        extra = in_a_box(holds, lambda ids: over_y(embed(ids)), tie(ids_by_step, r0)[0])
        r1, y0, extra = tie(r1, y0, extra)

        other = (3 * b, -3 * b)
        at_own = [(4 * b, 0, 0, 0, 0)]
        at_r = [None] + [[(3 * b, 0, k, 0, b)] for k in range(1, heads)]
        at_y = [[(3 * b, 1, k, 0, b)] for k in range(3)] + [[(2 * b, 1, 3, 0, 2 * b)]]
        at_x = [
            None,
            [(b, 0, 1, *other), (b, 1, 0, *other)],
            [(b, 0, 2, *other), (b, 1, 1, *other)],
            [(b, 0, 3, *other), (b, 1, 2, *other)],
            [(2 * b, 1, 3, 2 * b, -2 * b)],
        ]

        r2 = grid.send(r1, head=1)
        y1 = grid.send(r1, y=1)
        (edges,) = assemble([edge(r1), edge(y0)])
        x1 = grid.send(edges, side=1)

        def first_latents(*pieces):
            latent = add_pairs(swapped(pieces), [at_own, at_r[1], at_y[0]], None)
            return latent, r0[3 * b :], r1[3 * b :]

        latent, up0, up1 = in_a_box(holds, first_latents, tie(own, edges)[0], r1, y0)
        r2, y1, x1, latent, extra = tie(r2, y1, x1, latent, extra)

        r3 = grid.send(r2, head=1)
        y2 = grid.send(r2, y=1)
        (edges,) = assemble([edge(r2), edge(y1)])
        x2 = grid.send(edges, side=1)

        def second_latents(pieces, latent, lengths):
            latent = add_pairs(swapped(pieces), [at_r[2], at_y[1], at_x[1]], latent)
            return latent, make_turns(lengths), pieces[0][3 * b :]

        latent, turns, up2 = in_a_box(
            holds, second_latents, (r2, y1, x1), latent, tie(lengths, r2)[0]
        )
        r3, y2, x2, latent = tie(r3, y2, x2, latent)

        last, edges = assemble([(r3, 2 * b, 0, b)], [edge(r3), edge(y2)])
        y3 = grid.send(last, y=1)
        x3 = grid.send(edges, side=1)
        extra, last = tie(extra, last)

        def third_latents(pieces, latent, extra, *turns):
            extra = over_head(extra)
            latent = add_pairs(swapped(pieces), [at_r[3], at_y[2]], latent)
            extra, latent = tie(extra, latent)
            return latent, turn(extra, *turns), pieces[0][3 * b :]

        latent, extra, up3 = in_a_box(holds, third_latents, (r3, y2), latent, extra, *turns)
        x2, x3, y3, latent, extra = tie(x2, x3, y3, latent, extra)

        x4 = grid.send(y3, side=1)

        def fourth_latents(pieces, latent, extra):
            extra = spread_y(extra)
            pairs = swapped(pieces)
            extra, pairs = tie(extra, pairs)
            latent = add_pairs(pairs, [at_x[2], at_y[3], at_x[3]], latent)
            return latent, lay_out(spread(extra))

        latent, extra = in_a_box(holds, fourth_latents, (x2, y3, x3), latent, extra)
        x4, latent, extra = tie(x4, latent, extra)
        batch = list(zip((x4, grid.send(x4, core=1)), on_cores(*at_x[4])))
        return batch, latent, (extra, ([up0, up1, up2, up3], 0), turns)

    def project_plain(own, between):
        latent = None
        ring = own
        for k in range(heads):
            if k:
                ring = grid.send(ring, head=1)
            if k:
                latent = add_latents(hidden, depth, batch, latent)
            batch = both(ring, (depth, 0, k, 0, 0))
            for dy in range(1, ys):
                latent = add_latents(hidden, depth, batch, latent)
                batch = both(grid.send(ring, y=dy), (depth, dy, k, 0, 0))
        turns = make_turns(lengths)
        embed, over_y, over_head, turn, spread_y, spread, lay_out = between
        extra = turn(over_head(over_y(embed(ids_by_step))), *turns)
        extra = lay_out(spread(spread_y(extra)))
        ups = [pack_up(key_up)]
        ups += [grid.send(ups[0], head=k) for k in range(1, heads)]
        return batch, latent, (extra, (ups, 0), turns)

    blocks = 2 * ys * heads
    query_width = query_proj.shape[1] // blocks
    latent_width = down_proj.shape[1] // blocks
    cut = query_width + latent_width

    def embed(ids):
        keep, rest = pick(ids, embedding)
        keep, rest = new_sums(blocks, keep, grid.send(rest, side=1), query_proj, down_proj)
        packed = keep + grid.send(rest, core=1)
        return packed.reshape(ys, heads, rows, -1)

    def reduce_over_y(packed):
        kept = take(packed, y)
        for dy in range(1, ys):
            kept = kept + grid.send(take(packed, (y + dy) % ys), y=dy)
        return kept

    def reduce_over_head(kept):
        return lax.all_to_all(kept, "head", 0, 0)

    def turn(sums, cosine, sines):
        block = turn_query(sums, cosine, sines, query_width, latent_width)
        pair = in_order([block, grid.send(block, core=1)], c)
        return jnp.concatenate([pair[0], pair[1]], axis=-1)

    def spread_over_y(pair):
        return jnp.stack([pair] + [grid.send(pair, y=k) for k in range(1, ys)])

    def spread_over_head(by_y):
        return [by_y] + grid.along_heads(lambda k: by_y)

    def lay_out(by_head):
        return arrange(by_head, requests, query_width)

    pages = page_order.shape[1]
    start = ((y * 2 + c) * heads + z) * span

    def make_turns(lengths):
        fresh_positions = lengths[:, None] + jnp.arange(steps, dtype=jnp.int32)[None, :]
        positions = [
            start + PAGE * jnp.arange(pages, dtype=jnp.int32),
            jnp.arange(16 - pages % 16 if pages % 16 else 0, dtype=jnp.int32),
            jnp.arange(PAGE, dtype=jnp.int32),
            fresh_positions.reshape(-1),
        ]
        return sincos(jnp.concatenate(positions))

    between = [
        embed, reduce_over_y, reduce_over_head, turn, spread_over_y, spread_over_head, lay_out,
    ]
    shared = ys == 2 and heads == 4 and grid.sides == 2 and depth % 512 == 0
    batch, latent, extra = (project_shared if shared else project_plain)(down_proj, between)
    (queries, fresh), (ups, up_row), (cosine, sines) = extra
    weight = pltpu.with_memory_space_constraint(out_proj, pltpu.HBM)
    states, weight = finish(
        span, hidden, depth, batch, latent, fresh, cosine, sines, queries, ups, up_row, weight,
        heads, page_order, lengths, steps,
    )
    parts = [take(states, z)] + grid.along_heads(lambda k: take(states, (z + k) % heads))
    state = join_parts(parts)
    states = [state]
    for dy in range(ys - 1, -1, -1):
        for dc in (1, 0):
            if dy or dc:
                states.append(grid.send(state, y=dy, core=dc))
    partial_out = project_out(states, value_up, weight, requests, steps)
    sent = partial_out.astype(BF)
    attended = partial_out
    for part in grid.along_heads(lambda k: sent):
        attended = attended + part.astype(F32)
    return attended.astype(BF).reshape(requests, steps, -1)


def solution(mesh):
    return jax.shard_map(
        local,
        mesh=mesh,
        in_specs=(
            P("side", ("seq", "head"), None),
            P("side", ("seq", "head")),
            P("side"),
            P(),
            P("side", ("seq", "head")),
            P(("seq", "head"), None),
            P(("seq", "head"), None),
            P("head", None, None),
            P("head", None, None),
            P("head", "seq"),
        ),
        out_specs=P("side", None, "seq"),
        check_vma=False,
    )
```

```python
import functools
import math

import jax
import jax.numpy as jnp
from jax import lax
from jax.experimental import pallas as pl
from jax.experimental.pallas import tpu as pltpu
from jax.sharding import PartitionSpec as P

D = 8192
HQ = 64
KVH = 8
HD = 128
RANK = 64
PAGE = 16
FRESH = 16

AXES = ("side", "seq", "head")
rope_base = 500000.0
masked_score = -1e30
BF = jnp.bfloat16
F32 = jnp.float32


def sincos(positions):
    half = HD // 2
    frequency = 1.0 / rope_base ** (jnp.arange(half, dtype=F32) * 2.0 / HD)
    angles = positions.astype(F32)[..., None] * frequency
    cosine, sines = jnp.cos(angles), jnp.sin(angles)
    return (
        jnp.concatenate([cosine, cosine], axis=-1),
        jnp.concatenate([-sines, sines], axis=-1),
    )


class Grid:
    def __init__(self):
        self.sides, self.seqs, self.heads = (lax.axis_size(a) for a in AXES)
        self.ys = self.seqs // 2
        self.side, seq, self.z = (lax.axis_index(a) for a in AXES)
        self.y, self.c = lax.div(seq, 2), lax.rem(seq, 2)

    def send(self, value, side=0, y=0, core=0, head=0):
        pairs = []
        for a in range(self.sides):
            for b in range(self.ys):
                for c in range(2):
                    for d in range(self.heads):
                        to = (
                            (a + side) % self.sides,
                            (b + y) % self.ys,
                            (c + core) % 2,
                            (d + head) % self.heads,
                        )
                        pairs.append((self.flat(a, b, c, d), self.flat(*to)))
        return lax.ppermute(value, AXES, pairs)

    def along_heads(self, value_for):
        sent = {}
        for k in sorted(range(1, self.heads), key=lambda k: -min(k, self.heads - k)):
            sent[k] = self.send(value_for(k), head=k)
        return [sent[k] for k in range(1, self.heads)]

    def place(self, dy, dc, dz):
        seq = lax.rem(self.y + self.ys - dy, self.ys) * 2 + (1 - self.c if dc else self.c)
        return seq * self.heads + lax.rem(self.z + self.heads - dz, self.heads)

    def flat(self, a, b, c, d):
        return (a * self.seqs + b * 2 + c) * self.heads + d


def accumulate(
    counts, segments, depth, hidden_ref, pieces, before_ref, hidden_buf, piece_buf, total, sems, store=None
):
    grid = Grid()
    rows = hidden_ref.shape[0]
    if before_ref is not None:
        load = pltpu.make_async_copy(before_ref, total, sems.at[len(segments) + len(pieces)])
    waits = []
    at = 0
    for i, count in enumerate(counts):
        copies = [
            pltpu.make_async_copy(
                pieces[i].at[pl.ds(0, count), :],
                piece_buf.at[pl.ds(at, count), :],
                sems.at[len(segments) + i],
            )
        ]
        inside = 0
        for k, (owner, extent, dy, dc, dz, base, step) in enumerate(segments):
            if owner == i:
                source = grid.place(dy, dc, dz) * depth + base + step * grid.side
                source = pl.multiple_of(source, 128)
                copies.append(
                    pltpu.make_async_copy(
                        hidden_ref.at[:, pl.ds(source, extent)],
                        hidden_buf.at[:, pl.ds(at + inside, extent)],
                        sems.at[k],
                    )
                )
                inside += extent
        for copy in copies:
            copy.start()
        if before_ref is not None and i == 1:
            load.start()
        waits.append((copies, at, count))
        at += count
    pairs = [waits[i : i + 2] for i in range(0, len(waits), 2)]
    for k, pair in enumerate(pairs):
        for copies, _, _ in pair:
            for copy in copies:
                copy.wait()
        first = pair[0][1]
        span = sum(count for _, _, count in pair)
        last = k == len(pairs) - 1
        tile = rows // 4 if last and store else rows
        for m in range(rows // tile):
            part = slice(m * tile, (m + 1) * tile)
            term = jnp.dot(
                hidden_buf[part, first : first + span],
                piece_buf[first : first + span, :],
                preferred_element_type=F32,
            )
            if k == 0 and m == 0 and before_ref is not None:
                load.wait()
            total[part, :] = total[part, :] + term if k or before_ref is not None else term
            if last and store:
                store(m, tile)


def latent_kernel(counts, segments, depth, has_total, hidden_ref, *refs):
    pieces, refs = refs[: len(counts)], refs[len(counts) :]
    before_ref = None
    if has_total:
        before_ref, refs = refs[0], refs[1:]
    out_ref, hidden_buf, piece_buf, total, sems, out_sems = refs
    stores = []

    def store(m, tile):
        rows = pl.ds(m * tile, tile)
        copy = pltpu.make_async_copy(total.at[rows, :], out_ref.at[rows, :], out_sems.at[m])
        copy.start()
        stores.append(copy)

    accumulate(
        counts, segments, depth, hidden_ref, pieces, before_ref, hidden_buf, piece_buf, total, sems, store
    )
    for copy in stores:
        copy.wait()


def add_latents(hidden, depth, batch, total=None):
    pieces = [piece for piece, _ in batch]
    counts = [sum(part[0] for part in parts) for _, parts in batch]
    segments = [(i, *part) for i, (_, parts) in enumerate(batch) for part in parts]
    deep, columns = sum(counts), pieces[0].shape[1]
    rows = hidden.shape[0]
    operands = [hidden, *pieces]
    if total is not None:
        operands.append(total)
    return pl.pallas_call(
        functools.partial(latent_kernel, counts, segments, depth, total is not None),
        out_shape=jax.ShapeDtypeStruct((rows, columns), F32),
        in_specs=[pl.BlockSpec(memory_space=pl.ANY)] * len(operands),
        out_specs=pl.BlockSpec(memory_space=pl.ANY),
        scratch_shapes=[
            pltpu.VMEM((rows, deep), BF),
            pltpu.VMEM((deep, columns), BF),
            pltpu.VMEM((rows, columns), F32),
            pltpu.SemaphoreType.DMA((len(segments) + len(pieces) + 1,)),
            pltpu.SemaphoreType.DMA((4,)),
        ],
        compiler_params=pltpu.CompilerParams(vmem_limit_bytes=28 * 1024 * 1024),
        cost_estimate=pl.CostEstimate(
            flops=2 * rows * deep * columns,
            bytes_accessed=2 * deep * (rows + columns) + 8 * rows * columns,
            transcendentals=0,
        ),
        name="latents",
    )(*operands)


def first_piece_kernel(rows, own_ref, up_ref, out_ref, sems):
    side = lax.axis_index("side")
    groups = up_ref.shape[0]
    each = RANK // FRESH
    start = pl.multiple_of(rows * side, 16)
    copies = [
        pltpu.make_async_copy(
            own_ref.at[pl.ds(start, 3 * rows), :], out_ref.at[pl.ds(0, 3 * rows), :], sems.at[0]
        )
    ]
    for k in range(groups * each):
        copies.append(
            pltpu.make_async_copy(
                up_ref.at[k // each, pl.ds(k % each * FRESH, FRESH), :],
                out_ref.at[pl.ds(3 * rows, FRESH), pl.ds(k * HD, HD)],
                sems.at[1 + k],
            )
        )
    for copy in copies:
        copy.start()
    for copy in copies:
        copy.wait()


def first_piece(own, key_up, rows):
    count = key_up.shape[0] * RANK // FRESH
    return pl.pallas_call(
        functools.partial(first_piece_kernel, rows),
        out_shape=jax.ShapeDtypeStruct((3 * rows + FRESH, own.shape[1]), own.dtype),
        in_specs=[pl.BlockSpec(memory_space=pl.ANY)] * 2,
        out_specs=pl.BlockSpec(memory_space=pltpu.VMEM),
        scratch_shapes=[pltpu.SemaphoreType.DMA((1 + count,))],
        compiler_params=pltpu.CompilerParams(vmem_limit_bytes=8 * 1024 * 1024),
        cost_estimate=pl.CostEstimate(flops=1, bytes_accessed=1, transcendentals=0),
        name="first_piece",
    )(own, key_up)


def assemble_kernel(layout, *refs):
    ins, outs, sems = refs[: len(layout)], refs[len(layout) : -1], refs[-1]
    side = lax.axis_index("side")
    copies = []
    for k, (o, at, count, base, step) in enumerate(layout):
        start = pl.multiple_of(base + step * side, 16)
        copies.append(
            pltpu.make_async_copy(
                ins[k].at[pl.ds(start, count), :], outs[o].at[pl.ds(at, count), :], sems.at[k]
            )
        )
        copies[-1].start()
    for copy in copies:
        copy.wait()


def assemble(*arrays):
    layout, sources, shapes = [], [], []
    for o, parts in enumerate(arrays):
        at = 0
        for source, count, base, step in parts:
            layout.append((o, at, count, base, step))
            sources.append(source)
            at += count
        shapes.append(jax.ShapeDtypeStruct((at, source.shape[1]), source.dtype))
    return pl.pallas_call(
        functools.partial(assemble_kernel, layout),
        out_shape=shapes,
        in_specs=[pl.BlockSpec(memory_space=pl.ANY)] * len(sources),
        out_specs=[pl.BlockSpec(memory_space=pltpu.VMEM)] * len(shapes),
        scratch_shapes=[pltpu.SemaphoreType.DMA((len(layout),))],
        compiler_params=pltpu.CompilerParams(vmem_limit_bytes=8 * 1024 * 1024),
        cost_estimate=pl.CostEstimate(flops=1, bytes_accessed=1, transcendentals=0),
        name="assemble",
    )(*sources)


def in_three(value):
    high = value.astype(BF).astype(F32)
    middle = (value - high).astype(BF).astype(F32)
    return high, middle, value - high - middle


def pack_up(key_up):
    groups = key_up.shape[0]
    parts = key_up.reshape(groups, RANK // FRESH, FRESH, HD).transpose(2, 0, 1, 3)
    return parts.reshape(FRESH, -1)


def unpack_up(up_ref, g):
    each = up_ref.shape[2] // (RANK // FRESH * HD)
    at = g % each * (RANK // FRESH)
    parts = [up_ref[g // each, :, (at + i) * HD : (at + i + 1) * HD] for i in range(RANK // FRESH)]
    return jnp.concatenate(parts, axis=0)


def attend_part(scale, span, lat_ref, fresh_ref, cos_ref, sin_ref, live_ref, query_ref, up_ref, out_ref):
    requests, groups, lanes, _ = query_ref.shape
    blocks = out_ref.shape[0]
    each = groups // blocks
    peaks, totals, summed = [], [], []
    ups = [unpack_up(up_ref, g) for g in range(groups)]
    for r in range(requests):
        latent = jnp.concatenate(
            [
                lat_ref[r * span : (r + 1) * span, :].astype(BF),
                jnp.concatenate([fresh_ref[r, p] for p in range(fresh_ref.shape[1])], axis=1),
            ],
            axis=0,
        )
        cosine, sines = cos_ref[r], sin_ref[r]
        columns, values = [], []
        for g in range(groups):
            at = g * 2 * RANK
            key = jnp.dot(latent[:, at : at + RANK], ups[g], preferred_element_type=F32)
            key = (key * cosine + pltpu.roll(key, HD // 2, 1) * sines).astype(BF)
            columns.append(
                lax.dot_general(
                    key, query_ref[r, g], (((1,), (1,)), ((), ())), preferred_element_type=F32
                )
            )
            values.append(latent[:, at + RANK : at + 2 * RANK])
        scores = jnp.concatenate(columns, axis=1) * scale
        live = live_ref[r] > 0
        live = jnp.concatenate([live] * (scores.shape[1] // live.shape[1]), axis=1)
        scores = jnp.where(live, scores, masked_score)
        peak = jnp.max(scores, axis=0, keepdims=True)
        weights = jnp.where(live, jnp.exp(scores - peak), 0.0)
        peaks.append(peak)
        totals.append(jnp.sum(weights, axis=0, keepdims=True))
        summed.append(
            lax.dot_general(
                jnp.concatenate(values, axis=1),
                weights.astype(BF),
                (((0,), (0,)), ((), ())),
                preferred_element_type=F32,
            )
        )
    for b in range(blocks):
        stats = []
        for i in range(each):
            g = b * each + i
            cut = slice(g * lanes, (g + 1) * lanes)
            out_ref[b, i * RANK : (i + 1) * RANK, :] = jnp.concatenate(
                [s[g * RANK : (g + 1) * RANK, cut] for s in summed], axis=1
            ).astype(BF)
            stats += in_three(jnp.concatenate([p[:, cut] for p in peaks], axis=1))
            stats += in_three(jnp.concatenate([t[:, cut] for t in totals], axis=1))
        stats += [jnp.zeros_like(stats[0])] * (16 - len(stats))
        out_ref[b, each * RANK :, :] = jnp.concatenate(stats, axis=0).astype(BF)


def lay_tables(span, steps, start, order_ref, length_ref, small_cos, small_sin, cos_ref, sin_ref, live_ref):
    requests, rows, lanes = cos_ref.shape
    pages = order_ref.shape[1]
    padded = -(-pages // 16) * 16
    inner_cos, inner_sin = small_cos[padded : padded + PAGE, :], small_sin[padded : padded + PAGE, :]
    inner = lax.broadcasted_iota(jnp.int32, (PAGE, lanes), 0)
    grid = Grid()
    first = grid.place(0, 0, 0) == 0
    column_step = lax.rem(lax.broadcasted_iota(jnp.int32, (FRESH, lanes), 1), steps)
    new_row = lax.broadcasted_iota(jnp.int32, (FRESH, lanes), 0)
    seen = jnp.where(jnp.logical_and(new_row <= column_step, first), 1.0, 0.0)
    for j in range(pages):
        page_cos, page_sin = small_cos[j : j + 1, :], small_sin[j : j + 1, :]
        cosine = page_cos * inner_cos - page_sin * inner_sin
        sines = page_sin * inner_cos + page_cos * inner_sin
        for r in range(requests):
            at = pl.multiple_of(order_ref[r, j] * PAGE, PAGE)
            cos_ref[r, pl.ds(at, PAGE), :] = cosine
            sin_ref[r, pl.ds(at, PAGE), :] = sines
            position = start + j * PAGE + inner
            live_ref[r, pl.ds(at, PAGE), :] = jnp.where(position < length_ref[r], 1.0, 0.0)
    fill = jnp.zeros((FRESH - steps, lanes), F32)
    new = padded + PAGE
    for r in range(requests):
        own = slice(new + r * steps, new + (r + 1) * steps)
        cos_ref[r, span:, :] = jnp.concatenate([small_cos[own, :], fill], axis=0)
        sin_ref[r, span:, :] = jnp.concatenate([small_sin[own, :], fill], axis=0)
        live_ref[r, span:, :] = seen


def finish_kernel(counts, segments, depth, scale, span, up_row, steps, order_ref, length_ref, *refs):
    small_cos, small_sin, hidden_ref, refs = refs[0], refs[1], refs[2], refs[3:]
    pieces, refs = refs[: len(counts)], refs[len(counts) :]
    heads = lax.axis_size("head")
    before_ref, tables, ups, weight_ref = refs[0], refs[1:3], refs[3 : 3 + heads], refs[3 + heads]
    out_ref, weight_out, hidden_buf, piece_buf, total, *refs = refs[4 + heads :]
    held, (cos_ref, sin_ref, live_ref, up_buf, sems, table_sems, weight_sem) = refs[:2], refs[2:]
    loads = [
        pltpu.make_async_copy(table, buf, table_sems.at[i])
        for i, (table, buf) in enumerate(zip(tables, held))
    ]
    z = lax.axis_index("head")
    for k, up in enumerate(ups):
        place = lax.rem(z + heads - k, heads)
        loads.append(
            pltpu.make_async_copy(
                up.at[pl.ds(up_row, FRESH), :], up_buf.at[place], table_sems.at[len(tables) + k]
            )
        )
    for load in loads:
        load.start()
    grid = Grid()
    start = grid.place(0, 0, 0) * span
    lay_tables(
        span, steps, start, order_ref, length_ref, small_cos, small_sin, cos_ref, sin_ref, live_ref
    )
    accumulate(counts, segments, depth, hidden_ref, pieces, before_ref, hidden_buf, piece_buf, total, sems)
    for load in loads:
        load.wait()
    bring = pltpu.make_async_copy(weight_ref, weight_out, weight_sem)
    bring.start()
    fresh, queries = held
    attend_part(scale, span, total, fresh, cos_ref, sin_ref, live_ref, queries, up_buf, out_ref)
    bring.wait()


def finish(
    span, hidden, depth, batch, total, fresh, cosine, sines, queries, ups, up_row, weight, blocks,
    page_order, lengths, steps,
):
    pieces = [piece for piece, _ in batch]
    counts = [sum(part[0] for part in parts) for _, parts in batch]
    segments = [(i, *part) for i, (_, parts) in enumerate(batch) for part in parts]
    deep, columns = sum(counts), pieces[0].shape[1]
    rows = hidden.shape[0]
    requests, groups, lanes, _ = queries.shape
    tables = (fresh, queries)
    wide = (requests, span + FRESH, HD)
    total = pltpu.with_memory_space_constraint(total, pltpu.VMEM)
    operands = [page_order, lengths, cosine, sines, hidden, *pieces, total, *tables, *ups, weight]
    far = [pl.BlockSpec(memory_space=pl.ANY)] * (len(operands) - 4)
    state_rows = groups // blocks * RANK + 16
    return pl.pallas_call(
        functools.partial(
            finish_kernel, counts, segments, depth, 1.0 / math.sqrt(HD), span, up_row, steps
        ),
        out_shape=(
            jax.ShapeDtypeStruct((blocks, state_rows, requests * lanes), BF),
            pltpu.VMEM(weight.shape, weight.dtype),
        ),
        in_specs=[pl.BlockSpec(memory_space=pltpu.SMEM)] * 2
        + [pl.BlockSpec(memory_space=pltpu.VMEM)] * 2
        + far,
        out_specs=(pl.BlockSpec(memory_space=pltpu.VMEM), pl.BlockSpec(memory_space=pl.ANY)),
        scratch_shapes=[
            pltpu.VMEM((rows, deep), BF),
            pltpu.VMEM((deep, columns), BF),
            pltpu.VMEM((rows, columns), F32),
        ]
        + [pltpu.VMEM(table.shape, table.dtype) for table in tables]
        + [pltpu.VMEM(wide, F32)] * 3
        + [
            pltpu.VMEM((len(ups), FRESH, ups[0].shape[1]), BF),
            pltpu.SemaphoreType.DMA((len(segments) + len(pieces) + 1,)),
            pltpu.SemaphoreType.DMA((len(tables) + len(ups),)),
            pltpu.SemaphoreType.DMA,
        ],
        compiler_params=pltpu.CompilerParams(vmem_limit_bytes=18 * 1024 * 1024),
        cost_estimate=pl.CostEstimate(flops=1, bytes_accessed=1, transcendentals=0),
        name="finish",
    )(*operands)


def join(states):
    peak = functools.reduce(jnp.maximum, [p for p, _, _ in states])
    total, summed = 0.0, 0.0
    for p, t, s in states:
        weight = jnp.exp(p - peak)
        total = total + t * weight
        summed = summed + s * weight
    return peak, total, summed


def pack(states, out_ref):
    each = len(states)
    stats = []
    for i, (peak, total, summed) in enumerate(states):
        out_ref[i * RANK : (i + 1) * RANK, :] = summed.astype(BF)
        stats += [*in_three(peak), *in_three(total)]
    stats += [jnp.zeros_like(stats[0])] * (16 - len(stats))
    out_ref[each * RANK :, :] = jnp.concatenate(stats, axis=0).astype(BF)


def unpack(ref, each):
    stats = ref[each * RANK :, :].astype(F32)
    states = []
    for i in range(each):
        three = [stats[at : at + 1] for at in range(6 * i, 6 * i + 6)]
        peak, total = three[0] + three[1] + three[2], three[3] + three[4] + three[5]
        states.append((peak, total, ref[i * RANK : (i + 1) * RANK, :].astype(F32)))
    return states


def join_parts_kernel(each, *refs):
    refs, out_ref = refs[:-1], refs[-1]
    parts = [unpack(ref, each) for ref in refs]
    pack([join([part[i] for part in parts]) for i in range(each)], out_ref)


def join_parts(parts):
    return pl.pallas_call(
        functools.partial(join_parts_kernel, (parts[0].shape[0] - 16) // RANK),
        out_shape=jax.ShapeDtypeStruct(parts[0].shape, BF),
        compiler_params=pltpu.CompilerParams(vmem_limit_bytes=4 * 1024 * 1024),
        cost_estimate=pl.CostEstimate(flops=1, bytes_accessed=1, transcendentals=0),
        name="join_parts",
    )(*parts)


def project_out_kernel(requests, steps, *refs):
    up_ref, weight_ref, out_ref = refs[-3:]
    each = up_ref.shape[0]
    parts = [unpack(ref, each) for ref in refs[:-3]]
    lanes = refs[0].shape[1]
    rows = requests * steps
    heads = lanes // rows
    old = lax.broadcasted_iota(jnp.int32, (lanes, lanes), 0)
    new = lax.broadcasted_iota(jnp.int32, (lanes, lanes), 1)
    request, rest = old // (heads * steps), old % (heads * steps)
    moved = (rest // steps) * rows + request * steps + rest % steps
    order = jnp.where(moved == new, 1.0, 0.0).astype(BF)
    context = []
    for i in range(each):
        _, total, summed = join([part[i] for part in parts])
        scaled = (summed / total).astype(BF)
        one = lax.dot_general(
            up_ref[i], scaled, (((0,), (0,)), ((), ())), preferred_element_type=F32
        ).astype(BF)
        one = lax.dot_general(
            order, one, (((0,), (1,)), ((), ())), preferred_element_type=F32
        ).astype(BF)
        context += [one[j * rows : (j + 1) * rows, :] for j in range(heads)]
    total = jnp.dot(
        jnp.concatenate(context, axis=1), weight_ref[...], preferred_element_type=F32
    )
    for r in range(requests):
        out_ref[r] = total[r * steps : (r + 1) * steps, :]


def project_out(parts, value_up, out_proj, requests, steps):
    return pl.pallas_call(
        functools.partial(project_out_kernel, requests, steps),
        out_shape=jax.ShapeDtypeStruct((requests, steps, out_proj.shape[1]), F32),
        compiler_params=pltpu.CompilerParams(vmem_limit_bytes=24 * 1024 * 1024),
        cost_estimate=pl.CostEstimate(flops=1, bytes_accessed=1, transcendentals=0),
        name="project_out",
    )(*parts, value_up, out_proj)


def take(stack, index, axis=0):
    return lax.dynamic_index_in_dim(stack, index, axis, keepdims=False)


def tie(*values):
    leaves, tree = jax.tree.flatten(values)
    arrays = [i for i, leaf in enumerate(leaves) if getattr(leaf, "ndim", 0)]
    for i, leaf in zip(arrays, lax.optimization_barrier([leaves[i] for i in arrays])):
        leaves[i] = leaf
    return jax.tree.unflatten(tree, leaves)


def turn_query_kernel(query_width, latent_width, sums_ref, cos_ref, sin_ref, out_ref):
    sums = sums_ref[0]
    for k in range(1, sums_ref.shape[0]):
        sums = sums + sums_ref[k]
    at = query_width + latent_width
    sums = sums * lax.rsqrt(sums[:, at : at + 1] / D + 1e-05)
    own = slice(cos_ref.shape[0] - sums.shape[0], None)
    cosine, sines = cos_ref[own, :], sin_ref[own, :]
    for h in range(query_width // HD):
        one = sums[:, h * HD : (h + 1) * HD]
        one = one * cosine + pltpu.roll(one, HD // 2, 1) * sines
        out_ref[:, h * HD : (h + 1) * HD] = one.astype(BF)
    out_ref[:, query_width:at] = sums[:, query_width:at].astype(BF)


def turn_query(sums, cosine, sines, query_width, latent_width):
    return pl.pallas_call(
        functools.partial(turn_query_kernel, query_width, latent_width),
        out_shape=jax.ShapeDtypeStruct((sums.shape[1], query_width + latent_width), BF),
        compiler_params=pltpu.CompilerParams(vmem_limit_bytes=4 * 1024 * 1024),
        name="turn_query",
    )(sums, cosine, sines)


def pick_kernel(ids_ref, table_ref, keep_ref, send_ref, buf, sems):
    side = lax.axis_index("side")
    rows = table_ref.shape[0]
    steps, requests = ids_ref.shape
    count = requests * steps
    places = []
    for i in range(count):
        place = ids_ref[i % steps, i // steps] - side * rows
        inside = jnp.logical_and(place >= 0, place < rows)
        place = jnp.where(inside, place, 0)
        start = pl.multiple_of(lax.div(place, FRESH) * FRESH, FRESH)
        pltpu.make_async_copy(table_ref.at[pl.ds(start, FRESH), :], buf.at[i], sems.at[i]).start()
        places.append(jnp.where(inside, place - start, FRESH))
    row = lax.broadcasted_iota(jnp.int32, buf.shape[1:], 0)
    for half in range(2):
        picked = []
        for i in range(half * count // 2, (half + 1) * count // 2):
            pltpu.make_async_copy(table_ref.at[pl.ds(0, FRESH), :], buf.at[i], sems.at[i]).wait()
            one = jnp.where(row == places[i], buf[i].astype(F32), 0.0)
            picked.append(jnp.sum(one, axis=0, keepdims=True))
        picked = jnp.concatenate(picked, axis=0).astype(BF)

        @pl.when(side == half)
        def _():
            keep_ref[...] = picked

        @pl.when(side != half)
        def _():
            send_ref[...] = picked


def pick(ids, table):
    width = table.shape[1]
    half = jax.ShapeDtypeStruct((ids.size // 2, width), BF)
    return pl.pallas_call(
        pick_kernel,
        out_shape=(half, half),
        in_specs=[pl.BlockSpec(memory_space=pltpu.SMEM), pl.BlockSpec(memory_space=pl.ANY)],
        scratch_shapes=[
            pltpu.VMEM((ids.size, FRESH, width), BF),
            pltpu.SemaphoreType.DMA((ids.size,)),
        ],
        compiler_params=pltpu.CompilerParams(vmem_limit_bytes=4 * 1024 * 1024),
        name="pick",
    )(ids, table)


def new_sums_kernel(
    blocks, one_ref, other_ref, query_far, down_ref, keep_ref, send_ref, query_ref, sems
):
    wide = query_ref.shape[1] // sems.shape[0]
    copies = []
    for k in range(sems.shape[0]):
        part = pl.ds(k * wide, wide)
        copies.append(
            pltpu.make_async_copy(query_far.at[:, part], query_ref.at[:, part], sems.at[k])
        )
        copies[-1].start()
    core = lax.rem(lax.axis_index("seq"), 2)
    rows = one_ref[...] + other_ref[...]
    widened = rows.astype(F32)
    squares = jnp.sum(widened * widened, axis=1, keepdims=True)
    latents = jnp.dot(rows, down_ref[...], preferred_element_type=F32)
    query_width = query_ref.shape[1] // blocks
    latent_width = down_ref.shape[1] // blocks
    rest = 128 - latent_width
    for k in range(blocks):
        part = slice(k * query_width, (k + 1) * query_width)
        if k * query_width % wide == 0:
            copies[k * query_width // wide].wait()
        query = jnp.dot(rows, query_ref[:, part], preferred_element_type=F32)
        tail = jnp.concatenate(
            [
                latents[:, k * latent_width : (k + 1) * latent_width],
                jnp.broadcast_to(squares, (rows.shape[0], rest)),
            ],
            axis=1,
        )
        for same, ref in ((True, keep_ref), (False, send_ref)):

            @pl.when((core == k % 2) == same)
            def _(ref=ref, query=query, tail=tail):
                ref[k // 2, :, :query_width] = query
                ref[k // 2, :, query_width:] = tail


def new_sums(blocks, one, other, query_proj, down_proj):
    width = query_proj.shape[1] // blocks + 128
    half = jax.ShapeDtypeStruct((blocks // 2, one.shape[0], width), F32)
    return pl.pallas_call(
        functools.partial(new_sums_kernel, blocks),
        out_shape=(half, half),
        in_specs=[pl.BlockSpec(memory_space=pltpu.VMEM)] * 2
        + [pl.BlockSpec(memory_space=pl.ANY), pl.BlockSpec(memory_space=pltpu.VMEM)],
        scratch_shapes=[
            pltpu.VMEM(query_proj.shape, query_proj.dtype),
            pltpu.SemaphoreType.DMA((8,)),
        ],
        compiler_params=pltpu.CompilerParams(vmem_limit_bytes=20 * 1024 * 1024),
        name="new_sums",
    )(one, other, pltpu.with_memory_space_constraint(query_proj, pltpu.HBM), down_proj)


def arrange_kernel(query_width, *refs):
    refs, (query_ref, fresh_ref) = refs[:-2], refs[-2:]
    grid = Grid()
    ys, rows, width = refs[0].shape
    heads = len(refs)
    requests = query_ref.shape[0]
    steps = rows // requests
    cut = width // 2
    each = query_width // HD
    latent_width = cut - query_width
    fresh_ref[...] = jnp.zeros_like(fresh_ref)
    for dz, ref in enumerate(refs):
        for dy in range(ys):
            y = lax.rem(grid.y + ys - dy, ys)
            pair = y * heads + lax.rem(grid.z + heads - dz, heads)
            parts = 2 * each
            first = pair * parts
            g = lax.div(first, HQ // KVH)
            place = lax.rem(first, HQ // KVH) * steps
            for r in range(requests):
                own = []
                for h in range(parts):
                    at = h // each * cut + h % each * HD
                    own.append(ref[dy, r * steps : (r + 1) * steps, at : at + HD])
                start = pl.multiple_of(place, parts * steps)
                query_ref[r, g, pl.ds(start, parts * steps), :] = jnp.concatenate(own, axis=0)
            latents = [
                ref[dy, :, core * cut + query_width : (core + 1) * cut] for core in range(2)
            ]
            latents = jnp.concatenate(latents, axis=1)
            for r in range(requests):
                fresh_ref[r, pair, :steps, :] = latents[r * steps : (r + 1) * steps, :]


def arrange(by_head, requests, query_width):
    ys, rows, width = by_head[0].shape
    steps = rows // requests
    latents = width - 2 * query_width
    return pl.pallas_call(
        functools.partial(arrange_kernel, query_width),
        out_shape=(
            jax.ShapeDtypeStruct((requests, KVH, HQ // KVH * steps, HD), BF),
            jax.ShapeDtypeStruct((requests, ys * len(by_head), FRESH, latents), BF),
        ),
        compiler_params=pltpu.CompilerParams(vmem_limit_bytes=8 * 1024 * 1024),
        name="arrange",
    )(*by_head)


def in_a_box(holds, step, *values):
    shapes = jax.eval_shape(step, *values)

    def otherwise(*_):
        return jax.tree.map(lambda one: jnp.zeros(one.shape, one.dtype), shapes)

    return lax.cond(holds, step, otherwise, *values)


def in_order(parts, mine):
    count = len(parts)
    if count == 2:
        swap = mine == 0
        return jnp.stack([jnp.where(swap, parts[0], parts[1]), jnp.where(swap, parts[1], parts[0])])
    twice = jnp.stack(parts[::-1] * 2)
    return lax.dynamic_slice_in_dim(twice, count - 1 - mine, count, 0)


def local(
    cached_hidden,
    page_order,
    lengths,
    new_ids,
    embedding,
    query_proj,
    down_proj,
    key_up,
    value_up,
    out_proj,
):
    grid = Grid()
    side, y, c, z = grid.side, grid.y, grid.c, grid.z
    ys, heads = grid.ys, grid.heads
    requests, span, width = cached_hidden.shape
    tokens, steps = new_ids.shape
    rows = requests * steps
    depth = down_proj.shape[0]
    hidden = cached_hidden.reshape(requests * span, width)
    hidden = pltpu.with_memory_space_constraint(hidden, pltpu.HBM)
    ids_by_step = new_ids.T
    holds = ids_by_step[0, 0] >= 0

    def on_cores(*segments):
        return [
            [(rows, dy, dc, dz, base, step) for rows, dy, dz, base, step in segments]
            for dc in range(2)
        ]

    def both(piece, *segments):
        here, there = on_cores(*segments)
        return [(piece, here), (grid.send(piece, core=1), there)]

    def swapped(pieces, at_once=2):
        pairs = []
        for i, piece in enumerate(pieces):
            if i >= at_once:
                piece, _ = tie(piece, pairs[i - at_once][1])
            pairs.append((piece, grid.send(piece, core=1)))
        return pairs

    def add_pairs(pairs, places, latent):
        batch = []
        for pair, segments in zip(pairs, places):
            batch += list(zip(pair, on_cores(*segments)))
        return add_latents(hidden, depth, batch, latent)

    def project_shared(own, between):
        b = depth // 4

        def edge(piece):
            return piece, b, 0, 2 * b

        embed, over_y, over_head, turn, spread_y, spread, lay_out = between
        r0 = first_piece(own, key_up, b)
        r1 = grid.send(r0, head=1)
        y0 = grid.send(r0, y=1)

        extra = in_a_box(holds, lambda ids: over_y(embed(ids)), tie(ids_by_step, r0)[0])
        r1, y0, extra = tie(r1, y0, extra)

        other = (3 * b, -3 * b)
        at_own = [(4 * b, 0, 0, 0, 0)]
        at_r = [None] + [[(3 * b, 0, k, 0, b)] for k in range(1, heads)]
        at_y = [[(3 * b, 1, k, 0, b)] for k in range(3)] + [[(2 * b, 1, 3, 0, 2 * b)]]
        at_x = [
            None,
            [(b, 0, 1, *other), (b, 1, 0, *other)],
            [(b, 0, 2, *other), (b, 1, 1, *other)],
            [(b, 0, 3, *other), (b, 1, 2, *other)],
            [(2 * b, 1, 3, 2 * b, -2 * b)],
        ]

        r2 = grid.send(r1, head=1)
        y1 = grid.send(r1, y=1)
        (edges,) = assemble([edge(r1), edge(y0)])
        x1 = grid.send(edges, side=1)

        def first_latents(*pieces):
            latent = add_pairs(swapped(pieces), [at_own, at_r[1], at_y[0]], None)
            return latent, r0[3 * b :], r1[3 * b :]

        latent, up0, up1 = in_a_box(holds, first_latents, tie(own, edges)[0], r1, y0)
        r2, y1, x1, latent, extra = tie(r2, y1, x1, latent, extra)

        r3 = grid.send(r2, head=1)
        y2 = grid.send(r2, y=1)
        (edges,) = assemble([edge(r2), edge(y1)])
        x2 = grid.send(edges, side=1)

        def second_latents(pieces, latent, lengths):
            latent = add_pairs(swapped(pieces), [at_r[2], at_y[1], at_x[1]], latent)
            return latent, make_turns(lengths), pieces[0][3 * b :]

        latent, turns, up2 = in_a_box(
            holds, second_latents, (r2, y1, x1), latent, tie(lengths, r2)[0]
        )
        r3, y2, x2, latent = tie(r3, y2, x2, latent)

        last, edges = assemble([(r3, 2 * b, 0, b)], [edge(r3), edge(y2)])
        y3 = grid.send(last, y=1)
        x3 = grid.send(edges, side=1)
        extra, last = tie(extra, last)

        def third_latents(pieces, latent, extra, *turns):
            extra = over_head(extra)
            latent = add_pairs(swapped(pieces), [at_r[3], at_y[2]], latent)
            extra, latent = tie(extra, latent)
            return latent, turn(extra, *turns), pieces[0][3 * b :]

        latent, extra, up3 = in_a_box(holds, third_latents, (r3, y2), latent, extra, *turns)
        x2, x3, y3, latent, extra = tie(x2, x3, y3, latent, extra)

        x4 = grid.send(y3, side=1)

        def fourth_latents(pieces, latent, extra):
            extra = spread_y(extra)
            pairs = swapped(pieces)
            extra, pairs = tie(extra, pairs)
            latent = add_pairs(pairs, [at_x[2], at_y[3], at_x[3]], latent)
            return latent, lay_out(spread(extra))

        latent, extra = in_a_box(holds, fourth_latents, (x2, y3, x3), latent, extra)
        x4, latent, extra = tie(x4, latent, extra)
        batch = list(zip((x4, grid.send(x4, core=1)), on_cores(*at_x[4])))
        return batch, latent, (extra, ([up0, up1, up2, up3], 0), turns)

    def project_plain(own, between):
        latent = None
        ring = own
        for k in range(heads):
            if k:
                ring = grid.send(ring, head=1)
            if k:
                latent = add_latents(hidden, depth, batch, latent)
            batch = both(ring, (depth, 0, k, 0, 0))
            for dy in range(1, ys):
                latent = add_latents(hidden, depth, batch, latent)
                batch = both(grid.send(ring, y=dy), (depth, dy, k, 0, 0))
        turns = make_turns(lengths)
        embed, over_y, over_head, turn, spread_y, spread, lay_out = between
        extra = turn(over_head(over_y(embed(ids_by_step))), *turns)
        extra = lay_out(spread(spread_y(extra)))
        ups = [pack_up(key_up)]
        ups += [grid.send(ups[0], head=k) for k in range(1, heads)]
        return batch, latent, (extra, (ups, 0), turns)

    blocks = 2 * ys * heads
    query_width = query_proj.shape[1] // blocks
    latent_width = down_proj.shape[1] // blocks
    cut = query_width + latent_width

    def embed(ids):
        keep, rest = pick(ids, embedding)
        keep, rest = new_sums(blocks, keep, grid.send(rest, side=1), query_proj, down_proj)
        packed = keep + grid.send(rest, core=1)
        return packed.reshape(ys, heads, rows, -1)

    def reduce_over_y(packed):
        kept = take(packed, y)
        for dy in range(1, ys):
            kept = kept + grid.send(take(packed, (y + dy) % ys), y=dy)
        return kept

    def reduce_over_head(kept):
        return lax.all_to_all(kept, "head", 0, 0)

    def turn(sums, cosine, sines):
        block = turn_query(sums, cosine, sines, query_width, latent_width)
        pair = in_order([block, grid.send(block, core=1)], c)
        return jnp.concatenate([pair[0], pair[1]], axis=-1)

    def spread_over_y(pair):
        return jnp.stack([pair] + [grid.send(pair, y=k) for k in range(1, ys)])

    def spread_over_head(by_y):
        return [by_y] + grid.along_heads(lambda k: by_y)

    def lay_out(by_head):
        return arrange(by_head, requests, query_width)

    pages = page_order.shape[1]
    start = ((y * 2 + c) * heads + z) * span

    def make_turns(lengths):
        fresh_positions = lengths[:, None] + jnp.arange(steps, dtype=jnp.int32)[None, :]
        positions = [
            start + PAGE * jnp.arange(pages, dtype=jnp.int32),
            jnp.arange(16 - pages % 16 if pages % 16 else 0, dtype=jnp.int32),
            jnp.arange(PAGE, dtype=jnp.int32),
            fresh_positions.reshape(-1),
        ]
        return sincos(jnp.concatenate(positions))

    between = [
        embed, reduce_over_y, reduce_over_head, turn, spread_over_y, spread_over_head, lay_out,
    ]
    shared = ys == 2 and heads == 4 and grid.sides == 2 and depth % 512 == 0
    batch, latent, extra = (project_shared if shared else project_plain)(down_proj, between)
    (queries, fresh), (ups, up_row), (cosine, sines) = extra
    weight = pltpu.with_memory_space_constraint(out_proj, pltpu.HBM)
    states, weight = finish(
        span, hidden, depth, batch, latent, fresh, cosine, sines, queries, ups, up_row, weight,
        heads, page_order, lengths, steps,
    )
    parts = [take(states, z)] + grid.along_heads(lambda k: take(states, (z + k) % heads))
    state = join_parts(parts)
    states = [state]
    for dy in range(ys - 1, -1, -1):
        for dc in (1, 0):
            if dy or dc:
                states.append(grid.send(state, y=dy, core=dc))
    partial_out = project_out(states, value_up, weight, requests, steps)
    sent = partial_out.astype(BF)
    attended = partial_out
    for part in grid.along_heads(lambda k: sent):
        attended = attended + part.astype(F32)
    return attended.astype(BF)


def solution(mesh):
    return jax.shard_map(
        local,
        mesh=mesh,
        in_specs=(
            P("side", ("seq", "head"), None),
            P("side", ("seq", "head")),
            P("side"),
            P(),
            P("side", ("seq", "head")),
            P(("seq", "head"), None),
            P(("seq", "head"), None),
            P("head", None, None),
            P("head", None, None),
            P("head", "seq"),
        ),
        out_specs=P("side", None, "seq"),
        check_vma=False,
    )
```
